32 devices in a mesh: dom: 8 (over y, x, core), band: 4 (over z).
Axes of the slice: x: 2, y: 2, z: 4, core: 2. Of those that a mesh axis runs over, the one named last changes fastest.
Arguments:
- waves: float32 [2048, 2048], P('dom', 'band'), may hold values from -6 to 6
- cell_matrix: float32 [64, 125, 125], P('dom')
- connect: int32 [64, 125], P('dom'), may hold values from 0 to 383, as said below
- send_index: int32 [8, 2, 64], P('dom'), may hold values from 0 to 255
- rotation: float32 [2048, 2048], P('band'), may hold values from -0.125 to 0.125
Outputs:
- rotated: float32 [2048, 2048], P('dom', 'band')
The draws below stay inside these ranges and needn't reach their ends.
Inputs may be any that keep to these rules, and one draw needn't show every extreme that they name: On domain d, an entry of connect at or above 256 is 256 + k * 64 + s where s is below the number of slots that domain (d - 1 + 2 k) mod 8 fills on face k: exactly 64 for k = 1, between 64 // 2 (at least 1) and 64, uneven over domains, for k = 0; only those slots of send_index matter.
All inputs are finite; a program needn't handle non-finite values.
Results may differ from the reference program's by a relative error of at most 0.00012.
Values sent between devices are 32-bit elements; how exact they have to be, the bound alone decides.
A program may use at most 64 MiB of HBM per device.

```python
import jax
import jax.numpy as jnp
from jax import lax

BANDS = 2048
NPC = 125
DEGREE = 8
NOWN = 256
SLOT = 64
CELLS = 8
N_NODES = 2048
N_DOM = 8


def slot_counts(key):
    count_key = jax.random.fold_in(key, 7)
    lowest = max(1, SLOT // 2)
    uneven = jax.random.randint(count_key, (N_DOM,), lowest, SLOT + 1)
    full = jnp.full((N_DOM,), SLOT, jnp.int32)
    return jnp.stack([uneven.astype(jnp.int32), full], axis=1).astype(jnp.int32)


def draw_connect(key, part):
    counts = slot_counts(key)
    row_total = N_DOM * CELLS
    first, second, third, fourth = jax.random.split(jax.random.fold_in(key, 11), 4)
    device = (jnp.arange(row_total, dtype=jnp.int32) // CELLS)[:, None]
    device = jnp.broadcast_to(device, (row_total, NPC))
    ghost_pick = jax.random.randint(first, (row_total, NPC), 0, 4) == 0
    owned = jax.random.randint(second, (row_total, NPC), 0, NOWN)
    side = jax.random.randint(third, (row_total, NPC), 0, 2)
    source = (device - 1 + 2 * side) % N_DOM
    limit = counts[source, side]
    slot_pos = jax.random.randint(fourth, (row_total, NPC), 0, 1 << 20) % limit
    ghost = NOWN + side * SLOT + slot_pos
    result = jnp.where(ghost_pick, ghost, owned)
    cell_pos = jnp.arange(row_total, dtype=jnp.int32)[:, None] % CELLS
    column = jnp.arange(NPC, dtype=jnp.int32)[None, :]
    forced = NOWN + 2 * SLOT - 1
    result = jnp.where((cell_pos == 0) & (column == 0), forced, result)
    result = jnp.where((cell_pos == 0) & (column == 1), 0, result)
    return result.astype(jnp.int32)


def draw_cell_matrix(key, part):
    row_total = N_DOM * CELLS
    first, second = jax.random.split(jax.random.fold_in(key, 23), 2)
    raw = jax.random.normal(first, (row_total, NPC, NPC), jnp.float32)
    raw = raw * (0.6 / NPC ** 0.5)
    symmetric = (raw + jnp.swapaxes(raw, 1, 2)) * 0.70710678
    diagonal = jax.random.uniform(second, (row_total, NPC), jnp.float32, 0.5, 1.5)
    on_diag = jnp.arange(NPC)[:, None] == jnp.arange(NPC)[None, :]
    return jnp.where(on_diag[None, :, :], diagonal[:, :, None], symmetric).astype(jnp.float32)


def touch_ends(values, rng, smallest, largest):
    longest = values.shape.index(max(values.shape))
    spots = []
    for shift in (0, 1):
        where = [jax.random.randint(jax.random.fold_in(rng, axis), (), 0, length) for axis, length in enumerate(values.shape)]
        where[longest] = (where[longest] + shift) % values.shape[longest]
        spots.append(tuple(where))
    return values.at[spots[0]].set(smallest).at[spots[1]].set(largest)


def level_of(own_key, shape, pieces, least, high):
    level, own = 1.0, jax.random.fold_in(own_key, 6)
    for axis_at, parts in pieces:
        draws = jnp.exp(jax.random.uniform(jax.random.fold_in(own, axis_at), (parts,), jnp.float32, least / len(pieces), high / len(pieces)))
        level = level * jnp.repeat(draws, shape[axis_at] // parts).reshape([-1 if axis == axis_at else 1 for axis in range(len(shape))])
    return level


def noise(own_key, shape, spread, most, pieces=(), held_as=jnp.bfloat16):
    values = spread * jax.random.normal(own_key, shape, jnp.float32)
    if pieces:
        values = values * level_of(own_key, shape, pieces, -0.22, 0.18)
    return jnp.clip(values, -most, most).astype(held_as)


def setup_inputs(seed: int = 0) -> dict:
    seeds = jax.random.split(jax.random.key(seed), 6)
    waves = noise(seeds[0], (N_NODES, BANDS), 1.0, 6.0, ((0, 8), (1, 4)), jnp.float32)
    cell_matrix = draw_cell_matrix(jax.random.fold_in(seeds[5], 71), 0)
    connect = draw_connect(jax.random.fold_in(seeds[5], 71), 0)
    send_index = touch_ends(jax.random.randint(seeds[3], (N_DOM, 2, SLOT), 0, NOWN), jax.random.fold_in(seeds[3], 1), 0, NOWN - 1).astype(jnp.int32)
    rotation = noise(seeds[4], (BANDS, BANDS), BANDS ** -0.5, 0.125, ((0, 4),), jnp.float32)
    return dict(waves=waves, cell_matrix=cell_matrix, connect=connect, send_index=send_index, rotation=rotation)


centre = 5.5
half_width = 9.5


def assemble_ids(connect, send_index):
    device = (jnp.arange(connect.shape[0], dtype=jnp.int32) // CELLS)[:, None]
    device = jnp.broadcast_to(device, connect.shape).astype(jnp.int32)
    shifted = connect - NOWN
    is_ghost = shifted >= 0
    shifted = jnp.where(is_ghost, shifted, 0).astype(jnp.int32)
    side = (shifted // SLOT).astype(jnp.int32)
    slot_pos = (shifted % SLOT).astype(jnp.int32)
    source = ((device - 1 + 2 * side) % N_DOM).astype(jnp.int32)
    remote = source * NOWN + send_index[source, side, slot_pos]
    local = device * NOWN + connect
    return jnp.where(is_ghost, remote, local).astype(jnp.int32)


def operator_apply(vector, cell_matrix, global_ids):
    matrices = cell_matrix.reshape(N_DOM, CELLS, NPC, NPC)
    node_ids = global_ids.reshape(N_DOM, CELLS, NPC)

    def one_block(running, inputs):
        mats, block_ids = inputs
        gathered = vector[block_ids]
        product = jnp.einsum("cij,cjb->cib", mats, gathered, precision=lax.Precision.HIGHEST)
        running = running.at[block_ids.reshape(-1)].add(product.reshape(-1, vector.shape[1]))
        return running, None

    running, _ = lax.scan(one_block, jnp.zeros(vector.shape, jnp.float32), (matrices, node_ids))
    return running


def reference(waves, cell_matrix, connect, send_index, rotation):
    global_ids = assemble_ids(connect, send_index)
    previous = waves
    current = (operator_apply(waves, cell_matrix, global_ids) - centre * waves) / half_width
    for order in range(DEGREE - 1):
        image = operator_apply(current, cell_matrix, global_ids)
        following = 2.0 * (image - centre * current) / half_width - previous
        previous = current
        current = following
    return jnp.dot(current, rotation, precision=lax.Precision.HIGHEST, preferred_element_type=jnp.float32)
```

```python
import functools

import jax
import jax.numpy as jnp
from jax import lax
from jax.experimental import pallas as pl
from jax.experimental.pallas import tpu as pltpu
from jax.sharding import PartitionSpec as P

DEGREE = 8
LANES = 128
MESH = pl.DeviceIdType.MESH
CUTS = 4
ORDER = ((3, 0), (3, 1), (2, 0), (1, 0), (3, 2), (2, 1), (1, 1), (3, 3), (2, 2), (1, 2), (2, 3), (1, 3))


centre = 5.5
half_width = 9.5


def split(x):
    high = lax.reduce_precision(x, 8, 7)
    return high.astype(jnp.bfloat16), (x - high).astype(jnp.bfloat16)


def doubled(x, half):
    return x + pltpu.roll(x, half, 1)


def packed(x, half):
    high = x.astype(jnp.bfloat16)
    low = (x - high.astype(jnp.float32)).astype(jnp.bfloat16)
    lane = lax.broadcasted_iota(jnp.int32, x.shape, 1)
    return jnp.where(lane < half, high.astype(jnp.float32), low.astype(jnp.float32)).astype(
        jnp.bfloat16
    )


def mm(a, b):
    return jnp.dot(a, b, preferred_element_type=jnp.float32)


def filter_kernel(doms, owned, slots, half, high, low, pick, spread, start, out, pieces, ghosts, before, image):
    unroll = doms <= 8

    def over(body):
        if unroll:
            for d in range(doms):
                body(d)
        else:
            pl.loop(0, doms)(body)

    def begin(d):
        v = start[d]
        out[d] = v
        before[d] = jnp.zeros_like(v)
        pieces[d, :owned] = packed(v, half)

    over(begin)

    def one(step, _):
        def send(d):
            after = lax.rem(d + 1, doms) if not unroll else (d + 1) % doms
            ahead = lax.rem(d + doms - 1, doms) if not unroll else (d - 1) % doms
            g = mm(pick[d], pieces[d, :owned]).astype(jnp.bfloat16)
            pieces[after, owned : owned + slots] = g[:slots]
            pieces[ahead, owned + slots :] = g[slots:]

        over(send)

        def apply(d):
            x = pieces[d]
            y = mm(high[d], x) + mm(low[d], x)
            y = doubled(y, half)
            image[d] = y[:owned]
            after = lax.rem(d + 1, doms) if not unroll else (d + 1) % doms
            ahead = lax.rem(d + doms - 1, doms) if not unroll else (d - 1) % doms
            r = packed(y[owned:], half)
            ghosts[ahead, :slots] = r[:slots]
            ghosts[after, slots:] = r[slots:]

        over(apply)
        scale = jnp.where(step == 0, 1.0, 2.0)

        def update(d):
            y = image[d] + doubled(mm(spread[d], ghosts[d]), half)
            v = scale * y - before[d]
            before[d] = out[d]
            out[d] = v
            pieces[d, :owned] = packed(v, half)

        over(update)
        return 0

    lax.fori_loop(0, DEGREE, one, 0)


def high_low(x):
    high = x.astype(jnp.bfloat16)
    return high, (x - high.astype(jnp.float32)).astype(jnp.bfloat16)


def fused_kernel(bands, owned, slots, waves, cells, conn, send, rotation, out, *scratch):
    (acc, from_left, from_right, everyone, matrix, pick, spread, pieces, ghosts, image, even, odd,
     gathered, y_high, y_low, p_high, p_low,
     z_send, z_right, z_left, m_send, m_recv, y_send, y_recv) = scratch
    doms = 8
    size = owned + 2 * slots
    rows = owned // 2
    b16 = jnp.bfloat16
    me = lax.axis_index("dom")
    z = lax.axis_index("band")
    core = lax.rem(me, 2)
    place = lax.rem(lax.div(me, 2), 2)
    upper = lax.div(me, 4)
    sib = me + 1 - 2 * core
    x_next = me + 2 - 4 * place
    y_next = me + 4 - 8 * upper
    diag = x_next + 4 - 8 * upper
    across = x_next * (1 - core) + y_next * core
    onward = y_next * (1 - core) + x_next * core

    def seat_of(dom, at):
        return lax.rem(dom - at + doms, doms)

    barrier = pltpu.get_barrier_semaphore()
    for t in range(1, doms):
        pl.semaphore_signal(barrier, inc=1, device_id={"dom": lax.rem(me + t, doms)}, device_id_type=MESH)

    @pl.when(z > 0)
    def _():
        pl.semaphore_signal(barrier, inc=1, device_id={"band": z - 1}, device_id_type=MESH)

    @pl.when(z < bands - 1)
    def _():
        pl.semaphore_signal(barrier, inc=1, device_id={"band": z + 1}, device_id_type=MESH)

    beside = lax.div(z + bands - 1, bands) + lax.div(2 * bands - 2 - z, bands)
    pl.semaphore_wait(barrier, doms - 1 + beside)

    def to_right(j, c):
        return pltpu.make_async_remote_copy(
            src_ref=acc.at[j, c], dst_ref=from_left.at[j, c], send_sem=z_send.at[j, c],
            recv_sem=z_right.at[j, c], device_id={"band": z + 1}, device_id_type=MESH)

    def to_left(j, c):
        return pltpu.make_async_remote_copy(
            src_ref=acc.at[j, c], dst_ref=from_right.at[j, c], send_sem=z_send.at[j, c],
            recv_sem=z_left.at[j, c], device_id={"band": z - 1}, device_id_type=MESH)

    def send_right(items):
        @pl.when(z == 0)
        def _():
            for j, c in items:
                to_right(j, c).start()

    def send_left(items):
        @pl.when(z == bands - 1)
        def _():
            for j, c in items:
                to_left(bands - 1 - j, c).start()

    w_high, w_low = high_low(waves[...])
    width = waves.shape[1]

    def partial(j):
        r_high, r_low = high_low(rotation[:, j * width : (j + 1) * width])
        y = mm(w_high, r_high) + (mm(w_high, r_low) + mm(w_low, r_high))
        for c in range(CUTS):
            acc[j, c] = y[:, c * LANES : (c + 1) * LANES]

    partial(3)
    send_right(ORDER[:2])
    partial(0)
    send_left(ORDER[:2])

    node = lax.broadcasted_iota(jnp.int32, (size, conn.shape[1]), 0)
    total = jnp.zeros((size, size), jnp.float32)
    for c in range(cells.shape[1]):
        seat = jnp.where(node == conn[c : c + 1, :], 1.0, 0.0).astype(b16)
        a_high, a_low = high_low(cells[:, c, :])
        b_high, b_low = high_low(mm(seat, a_high) + mm(seat, a_low))
        dims = (((1,), (1,)), ((), ()))
        total = total + (
            lax.dot_general(b_high, seat, dims, preferred_element_type=jnp.float32)
            + lax.dot_general(b_low, seat, dims, preferred_element_type=jnp.float32))
    r_at = lax.broadcasted_iota(jnp.int32, (size, size), 0)
    c_at = lax.broadcasted_iota(jnp.int32, (size, size), 1)
    shift = jnp.where((r_at == c_at) & (r_at < owned), centre, 0.0)
    total = (total - shift) / half_width
    everyone[0, :rows] = total[:rows]
    everyone[0, rows:owned, rows:] = total[rows:owned, rows:]
    everyone[0, rows:owned, :rows] = total[owned:, owned:]
    everyone[0, owned:] = jnp.zeros((8, size), jnp.float32)
    everyone[0, owned : owned + 2, :slots] = send[0].astype(jnp.float32)

    def m_copy(dom, to, k):
        return pltpu.make_async_remote_copy(
            src_ref=everyone.at[seat_of(dom, me)], dst_ref=everyone.at[seat_of(dom, to)], send_sem=m_send.at[k],
            recv_sem=m_recv.at[seat_of(dom, to)], device_id={"dom": to}, device_id_type=MESH)

    def m_wait(dom):
        pltpu.make_async_remote_copy(
            src_ref=everyone.at[0], dst_ref=everyone.at[seat_of(dom, me)], send_sem=m_send.at[0],
            recv_sem=m_recv.at[seat_of(dom, me)], device_id={"dom": sib}, device_id_type=MESH).wait_recv()

    def y_copy(c, dom, to, k):
        return pltpu.make_async_remote_copy(
            src_ref=gathered.at[seat_of(dom, me), c], dst_ref=gathered.at[seat_of(dom, to), c],
            send_sem=y_send.at[c, k], recv_sem=y_recv.at[c, seat_of(dom, to)], device_id={"dom": to},
            device_id_type=MESH)

    def y_wait(c, dom):
        pltpu.make_async_remote_copy(
            src_ref=gathered.at[0, c], dst_ref=gathered.at[seat_of(dom, me), c], send_sem=y_send.at[c, 0],
            recv_sem=y_recv.at[c, seat_of(dom, me)], device_id={"dom": sib}, device_id_type=MESH).wait_recv()

    unsent = []

    def go(copy):
        copy.start()
        unsent.append(copy)

    def first_hop(copy):
        go(copy(me, x_next, 0))
        go(copy(me, y_next, 1))
        go(copy(me, sib, 2))

    def second_hop(copy, wait):
        wait(x_next)
        wait(y_next)
        go(copy(across, onward, 3))
        go(copy(x_next, sib, 4))
        go(copy(y_next, sib, 5))

    def third_hop(copy, wait):
        wait(diag)
        go(copy(diag, sib, 6))

    away = [sib, x_next + 1 - 2 * core, y_next + 1 - 2 * core, diag + 1 - 2 * core]

    first_hop(m_copy)

    partial(2)
    partial(1)
    send_right(ORDER[2:])
    send_left(ORDER[2:])

    def relay(k):
        def right(j, c):
            to_right(j, c).wait_recv()
            acc[j, c] = acc[j, c] + from_left[j, c]
            to_right(j, c).start()

        def left(j, c):
            to_left(j, c).wait_recv()
            acc[j, c] = acc[j, c] + from_right[j, c]
            to_left(j, c).start()

        last = bands - 1
        for hop in (1, 2):
            at = k - hop + 1
            if not 0 <= at < len(ORDER):
                continue
            j, c = ORDER[at]
            if j > hop:
                @pl.when(z == hop)
                def _():
                    right(j, c)

                @pl.when(z == last - hop)
                def _():
                    left(last - j, c)

    def finish(c):
        gathered[0, c] = acc[z, c]

        @pl.when(z > 0)
        def _():
            to_right(z, c).wait_recv()
            gathered[0, c] = gathered[0, c] + from_left[z, c]

        @pl.when(z < bands - 1)
        def _():
            to_left(z, c).wait_recv()
            gathered[0, c] = gathered[0, c] + from_right[z, c]

        first_hop(functools.partial(y_copy, c))

    def y_second(c):
        second_hop(functools.partial(y_copy, c), functools.partial(y_wait, c))

    def y_third(c):
        third_hop(functools.partial(y_copy, c), functools.partial(y_wait, c))

    def y_split(c):
        for dom in away:
            y_wait(c, dom)
        columns = slice(c * LANES, (c + 1) * LANES)
        for d in range(doms):
            high, low = high_low(gathered[d, c])
            y_high[d * owned : (d + 1) * owned, columns] = high
            y_low[d * owned : (d + 1) * owned, columns] = low

    def prepare(d):
        upper_rows = everyone[d, :rows]
        middle = everyone[d, rows:owned]
        whole = jnp.concatenate([
            upper_rows,
            jnp.concatenate([jnp.transpose(upper_rows[:, rows:owned]), middle[:, rows:]], axis=1),
            jnp.concatenate([
                jnp.transpose(upper_rows[:, owned:]), jnp.transpose(middle[:, owned:]),
                middle[:, :rows]], axis=1)], axis=0)
        m_high, m_low = high_low(whole)
        matrix[d, :, :size] = m_high
        matrix[d, :, size : 2 * size] = m_low
        matrix[d, :, 2 * size :] = m_high
        tile = everyone[d, owned:, :LANES]
        other = pltpu.roll(tile, slots, 1)
        first_lanes = lax.broadcasted_iota(jnp.int32, (1, LANES), 1) < slots
        row = jnp.where(first_lanes, tile[0:1], other[1:2]).astype(jnp.int32)
        at = lax.broadcasted_iota(jnp.int32, (owned, LANES), 0)
        hot = jnp.where(at == row, 1.0, 0.0)
        spread[d, :, :LANES] = hot.astype(b16)
        spread[d, :, LANES:] = hot.astype(b16)
        pick[d] = jnp.transpose(hot).astype(b16)

    pieces[...] = jnp.zeros_like(pieces)
    ghosts[...] = jnp.zeros_like(ghosts)
    i_at = lax.broadcasted_iota(jnp.int32, (owned, owned), 0)
    j_at = lax.broadcasted_iota(jnp.int32, (owned, owned), 1)
    eye = jnp.where(i_at == j_at, 1.0, 0.0)
    even[0] = eye
    pieces[0, :owned] = eye.astype(b16)
    pieces[0, size : size + owned] = eye.astype(b16)
    prepare(0)

    relay(0)
    relay(1)
    relay(2)
    second_hop(m_copy, m_wait)
    relay(3)
    finish(0)
    relay(4)
    third_hop(m_copy, m_wait)
    for dom in away:
        m_wait(dom)
    for d in range(1, doms):
        prepare(d)
    relay(5)

    every = list(range(doms))
    held = [[0], [6, 7, 0, 1, 2]]
    busy = [[7, 0, 1], [5, 6, 7, 0, 1, 2, 3]]

    def advance(k, end):
        source = held[k - 1] if k <= 2 else every
        active = busy[k - 1] if k <= 2 else every
        result = held[k] if k < 2 else every
        old = [] if k == 1 else held[k - 2] if k <= 3 else every
        store = odd if k % 2 else even
        for d in source:
            after, ahead = (d + 1) % doms, (d - 1) % doms
            for at, bases in ((0, (0, size)), (2 * size, (2 * size,))):
                g = mm(pick[d], pieces[d, at : at + owned]).astype(b16)
                for base in bases:
                    pieces[after, base + owned : base + owned + slots] = g[:slots]
                    pieces[ahead, base + owned + slots : base + size] = g[slots:]
        for d in active:
            after, ahead = (d + 1) % doms, (d - 1) % doms
            y = mm(matrix[d], pieces[d])
            image[d] = y[:owned]
            high, low = high_low(y[owned:])
            ghosts[ahead, :slots] = high[:slots]
            ghosts[ahead, 2 * slots : 3 * slots] = low[:slots]
            ghosts[after, slots : 2 * slots] = high[slots:]
            ghosts[after, 3 * slots :] = low[slots:]
        for d in result:
            y = mm(spread[d], ghosts[d])
            if d in active:
                y = y + image[d]
            v = y if k == 1 else 2.0 * y
            if d in old:
                v = v - store[d]
            if end:
                high, low = high_low(jnp.transpose(v))
                p_high[:, d * owned : (d + 1) * owned] = high
                p_low[:, d * owned : (d + 1) * owned] = low
            else:
                store[d] = v
                high, low = high_low(v)
                pieces[d, :owned] = high
                pieces[d, size : size + owned] = high
                pieces[d, 2 * size : 2 * size + owned] = low

    advance(1, False)
    y_second(0)
    relay(6)
    finish(1)
    advance(2, False)
    relay(7)
    y_third(0)
    advance(3, False)
    relay(8)
    y_second(1)
    y_split(0)
    advance(4, False)
    relay(9)
    finish(2)
    y_third(1)
    advance(5, False)
    relay(10)
    y_second(2)
    y_split(1)
    advance(6, False)
    relay(11)
    finish(3)
    y_third(2)
    advance(7, False)
    relay(12)
    y_second(3)
    y_split(2)
    advance(8, True)
    y_third(3)
    y_split(3)
    for h in range(width // owned):
        columns = slice(h * owned, (h + 1) * owned)
        high, low = y_high[:, columns], y_low[:, columns]
        out[:, columns] = mm(p_high[...], high) + (mm(p_high[...], low) + mm(p_low[...], high))

    for copy in unsent:
        copy.wait_send()
    for j in range(bands):
        for c in range(CUTS):
            @pl.when(z < j)
            def _():
                to_right(j, c).wait_send()

            @pl.when(z > j)
            def _():
                to_left(j, c).wait_send()


def fused(waves, cell_matrix, connect, send_index, rotation):
    owned, width = waves.shape
    slots = send_index.shape[2]
    bands = lax.axis_size("band")
    size = owned + 2 * slots
    doms = 8
    vmem = pl.BlockSpec(memory_space=pltpu.VMEM)
    f32, b16 = jnp.float32, jnp.bfloat16
    dma = pltpu.SemaphoreType.DMA
    return pl.pallas_call(
        functools.partial(fused_kernel, bands, owned, slots),
        out_shape=jax.ShapeDtypeStruct((owned, width), f32),
        in_specs=[vmem] * 5,
        out_specs=vmem,
        scratch_shapes=[
            pltpu.VMEM((bands, CUTS, owned, LANES), f32),
            pltpu.VMEM((bands, CUTS, owned, LANES), f32),
            pltpu.VMEM((bands, CUTS, owned, LANES), f32),
            pltpu.VMEM((doms, owned + 8, size), f32),
            pltpu.VMEM((doms, size, 3 * size), b16),
            pltpu.VMEM((doms, 2 * slots, owned), b16),
            pltpu.VMEM((doms, owned, 4 * slots), b16),
            pltpu.VMEM((doms, 3 * size, owned), b16),
            pltpu.VMEM((doms, 4 * slots, owned), b16),
            pltpu.VMEM((doms, owned, owned), f32),
            pltpu.VMEM((doms, owned, owned), f32),
            pltpu.VMEM((doms, owned, owned), f32),
            pltpu.VMEM((doms, CUTS, owned, LANES), f32),
            pltpu.VMEM((doms * owned, width), b16),
            pltpu.VMEM((doms * owned, width), b16),
            pltpu.VMEM((owned, doms * owned), b16),
            pltpu.VMEM((owned, doms * owned), b16),
            dma((bands, CUTS)), dma((bands, CUTS)), dma((bands, CUTS)),
            dma((7,)), dma((doms,)),
            dma((CUTS, 7)), dma((CUTS, doms)),
        ],
        compiler_params=pltpu.CompilerParams(
            vmem_limit_bytes=60 * 2**20, collective_id=0, has_side_effects=True),
        cost_estimate=pl.CostEstimate(
            flops=DEGREE * doms * 6 * size * size * owned, bytes_accessed=2**24, transcendentals=0),
    )(waves, jnp.swapaxes(cell_matrix, 0, 1), connect, send_index, rotation)


def shards(waves, cell_matrix, connect, send_index, rotation):
    owned = waves.shape[0]
    width = waves.shape[1]
    slots = send_index.shape[2]
    doms = lax.axis_size("dom")
    if doms == 8 and width == doms * LANES // 2 and 2 * slots == LANES and owned == 2 * LANES and lax.axis_size("band") == 4:
        return fused(waves, cell_matrix, connect, send_index, rotation)
    size = owned + 2 * slots
    seat = jax.nn.one_hot(connect, size, dtype=jnp.float32)
    half_way = jnp.einsum("cij,cjn->cin", cell_matrix, seat, precision=lax.Precision.HIGH)
    local = jnp.einsum("cim,cin->mn", seat, half_way, precision=lax.Precision.HIGH)
    node = jnp.arange(size)
    shift = jnp.where((node[:, None] == node[None, :]) & (node[:, None] < owned), centre, 0.0)
    local = (local - shift) / half_width
    row = jnp.zeros((8, size), jnp.float32).at[0, : 2 * slots].set(
        send_index.reshape(-1).astype(jnp.float32)
    )
    everyone = lax.all_gather(jnp.concatenate([local, row], axis=0), "dom")
    high, low = split(everyone[:, :size])
    index = everyone[:, size, : 2 * slots].astype(jnp.int32)
    pick = jax.nn.one_hot(index, owned, dtype=jnp.bfloat16)
    spread = jnp.swapaxes(pick, 1, 2)

    partial = jnp.dot(waves, rotation, precision=lax.Precision.HIGH, preferred_element_type=jnp.float32)
    turned = lax.psum_scatter(partial, "band", scatter_dimension=1, tiled=True)
    share = width // doms
    columns = lax.all_to_all(turned, "dom", split_axis=1, concat_axis=0, tiled=True)
    columns = columns.reshape(doms, owned, share)
    half = LANES // 2
    columns = jnp.pad(columns, ((0, 0), (0, 0), (0, half - share)))
    columns = jnp.concatenate([columns, columns], axis=2)
    vmem = pl.BlockSpec(memory_space=pltpu.VMEM)
    done = pl.pallas_call(
        functools.partial(filter_kernel, doms, owned, slots, half),
        out_shape=jax.ShapeDtypeStruct((doms, owned, LANES), jnp.float32),
        in_specs=[vmem] * 5,
        out_specs=vmem,
        scratch_shapes=[
            pltpu.VMEM((doms, size, LANES), jnp.bfloat16),
            pltpu.VMEM((doms, 2 * slots, LANES), jnp.bfloat16),
            pltpu.VMEM((doms, owned, LANES), jnp.float32),
            pltpu.VMEM((doms, owned, LANES), jnp.float32),
        ],
        compiler_params=pltpu.CompilerParams(vmem_limit_bytes=56 * 2**20),
        cost_estimate=pl.CostEstimate(
            flops=DEGREE * doms * 4 * size * size * LANES, bytes_accessed=2**24, transcendentals=0
        ),
    )(high, low, pick, spread, columns)
    back = done[:, :, :share].reshape(doms * owned, share)
    return lax.all_to_all(back, "dom", split_axis=0, concat_axis=1, tiled=True)


def solution(mesh):
    in_specs = (
        P("dom", "band"),
        P("dom", None, None),
        P("dom", None),
        P("dom", None, None),
        P("band", None),
    )
    out_specs = P("dom", "band")
    return jax.shard_map(shards, mesh=mesh, in_specs=in_specs, out_specs=out_specs, check_vma=False)
```

```python
import functools

import jax
import jax.numpy as jnp
from jax import lax
from jax.experimental import pallas as pl
from jax.experimental.pallas import tpu as pltpu
from jax.sharding import PartitionSpec as P

DEGREE = 8
LANES = 128
MESH = pl.DeviceIdType.MESH
SPAN = ((0, 64), (64, 64), (128, 64), (192, 32), (224, 32))
ORDER = ((3, 0), (3, 1), (2, 0), (1, 0), (3, 2), (2, 1), (1, 1), (3, 3), (2, 2), (1, 2), (3, 4), (2, 3), (2, 4),
         (1, 3), (1, 4))
HALVES = ((0, 104), (104, 96))


centre = 5.5
half_width = 9.5


def split(x):
    high = lax.reduce_precision(x, 8, 7)
    return high.astype(jnp.bfloat16), (x - high).astype(jnp.bfloat16)


def doubled(x, half):
    return x + pltpu.roll(x, half, 1)


def packed(x, half):
    high = x.astype(jnp.bfloat16)
    low = (x - high.astype(jnp.float32)).astype(jnp.bfloat16)
    lane = lax.broadcasted_iota(jnp.int32, x.shape, 1)
    return jnp.where(lane < half, high.astype(jnp.float32), low.astype(jnp.float32)).astype(
        jnp.bfloat16
    )


def mm(a, b):
    return jnp.dot(a, b, preferred_element_type=jnp.float32)


def filter_kernel(doms, owned, slots, half, high, low, pick, spread, start, out, pieces, ghosts, before, image):
    unroll = doms <= 8

    def over(body):
        if unroll:
            for d in range(doms):
                body(d)
        else:
            pl.loop(0, doms)(body)

    def begin(d):
        v = start[d]
        out[d] = v
        before[d] = jnp.zeros_like(v)
        pieces[d, :owned] = packed(v, half)

    over(begin)

    def one(step, _):
        def send(d):
            after = lax.rem(d + 1, doms) if not unroll else (d + 1) % doms
            ahead = lax.rem(d + doms - 1, doms) if not unroll else (d - 1) % doms
            g = mm(pick[d], pieces[d, :owned]).astype(jnp.bfloat16)
            pieces[after, owned : owned + slots] = g[:slots]
            pieces[ahead, owned + slots :] = g[slots:]

        over(send)

        def apply(d):
            x = pieces[d]
            y = mm(high[d], x) + mm(low[d], x)
            y = doubled(y, half)
            image[d] = y[:owned]
            after = lax.rem(d + 1, doms) if not unroll else (d + 1) % doms
            ahead = lax.rem(d + doms - 1, doms) if not unroll else (d - 1) % doms
            r = packed(y[owned:], half)
            ghosts[ahead, :slots] = r[:slots]
            ghosts[after, slots:] = r[slots:]

        over(apply)
        scale = jnp.where(step == 0, 1.0, 2.0)

        def update(d):
            y = image[d] + doubled(mm(spread[d], ghosts[d]), half)
            v = scale * y - before[d]
            before[d] = out[d]
            out[d] = v
            pieces[d, :owned] = packed(v, half)

        over(update)
        return 0

    lax.fori_loop(0, DEGREE, one, 0)


def high_low(x):
    high = x.astype(jnp.bfloat16)
    return high, (x - high.astype(jnp.float32)).astype(jnp.bfloat16)


def fused_kernel(bands, owned, slots, waves_in, cells_in, conn, send, rotation_in, out, *scratch):
    (waves, cells, rotation, load, acc, from_left, from_right, everyone, matrix, pick, spread, pieces, ghosts, image, even, odd,
     gathered, y_high, y_low, p_high, p_low,
     z_send, z_right, z_left, m_send, m_recv, y_send, y_recv) = scratch
    doms = 8
    size = owned + 2 * slots
    rows = owned // 2
    b16 = jnp.bfloat16
    me = lax.axis_index("dom")
    z = lax.axis_index("band")
    core = lax.rem(me, 2)
    place = lax.rem(lax.div(me, 2), 2)
    upper = lax.div(me, 4)
    sib = me + 1 - 2 * core
    x_next = me + 2 - 4 * place
    y_next = me + 4 - 8 * upper
    diag = x_next + 4 - 8 * upper
    across = x_next * (1 - core) + y_next * core
    onward = y_next * (1 - core) + x_next * core

    def seat_of(dom, at):
        return lax.rem(dom - at + doms, doms)

    barrier = pltpu.get_barrier_semaphore()
    for t in range(1, doms):
        pl.semaphore_signal(barrier, inc=1, device_id={"dom": lax.rem(me + t, doms)}, device_id_type=MESH)

    @pl.when(z > 0)
    def _():
        pl.semaphore_signal(barrier, inc=1, device_id={"band": z - 1}, device_id_type=MESH)

    @pl.when(z < bands - 1)
    def _():
        pl.semaphore_signal(barrier, inc=1, device_id={"band": z + 1}, device_id_type=MESH)

    width = waves.shape[1]

    def block(j):
        return pl.ds(j * width, width)

    order = []
    for r in range(bands // 2):
        order += [bands - 1 - r, r]
    loads = [pltpu.make_async_copy(waves_in, waves, load.at[bands + 1])]
    loads += [pltpu.make_async_copy(rotation_in.at[:, block(j)], rotation.at[:, block(j)], load.at[j]) for j in order]
    loads.insert(3, pltpu.make_async_copy(cells_in, cells, load.at[bands]))
    for copy in loads:
        copy.start()

    def rows_of(c):
        return pl.ds(*SPAN[c])

    def to_right(j, c):
        return pltpu.make_async_remote_copy(
            src_ref=acc.at[j, rows_of(c)], dst_ref=from_left.at[j, rows_of(c)], send_sem=z_send.at[j, c],
            recv_sem=z_right.at[j, c], device_id={"band": z + 1}, device_id_type=MESH)

    def to_left(j, c):
        return pltpu.make_async_remote_copy(
            src_ref=acc.at[j, rows_of(c)], dst_ref=from_right.at[j, rows_of(c)], send_sem=z_send.at[j, c],
            recv_sem=z_left.at[j, c], device_id={"band": z - 1}, device_id_type=MESH)

    def send_right(items):
        @pl.when(z == 0)
        def _():
            for j, c in items:
                to_right(j, c).start()

    def send_left(items):
        @pl.when(z == bands - 1)
        def _():
            for j, c in items:
                to_left(bands - 1 - j, c).start()

    loads[0].wait()
    w_high, w_low = high_low(waves[...])

    def partial(j):
        r_high, r_low = high_low(rotation[:, j * width : (j + 1) * width])
        acc[j] = mm(w_high, r_high) + (mm(w_high, r_low) + mm(w_low, r_high))

    loads[1].wait()
    partial(3)
    loads[2].wait()
    partial(0)
    beside = lax.div(z + bands - 1, bands) + lax.div(2 * bands - 2 - z, bands)
    pl.semaphore_wait(barrier, doms - 1 + beside)

    send_right(ORDER[:2])
    send_left(ORDER[:2])

    loads[3].wait()
    node = lax.broadcasted_iota(jnp.int32, (size, conn.shape[1]), 0)
    total = jnp.zeros((size, size), jnp.float32)
    for c in range(cells.shape[1]):
        seat = jnp.where(node == conn[c : c + 1, :], 1.0, 0.0).astype(b16)
        a_high, a_low = high_low(cells[:, c, :])
        b_high, b_low = high_low(mm(seat, a_high) + mm(seat, a_low))
        dims = (((1,), (1,)), ((), ()))
        total = total + (
            lax.dot_general(b_high, seat, dims, preferred_element_type=jnp.float32)
            + lax.dot_general(b_low, seat, dims, preferred_element_type=jnp.float32))
    r_at = lax.broadcasted_iota(jnp.int32, (size, size), 0)
    c_at = lax.broadcasted_iota(jnp.int32, (size, size), 1)
    shift = jnp.where((r_at == c_at) & (r_at < owned), centre, 0.0)
    total = (total - shift) / half_width
    i_at = lax.broadcasted_iota(jnp.int32, (rows, rows), 0)
    j_at = lax.broadcasted_iota(jnp.int32, (rows, rows), 1)
    quarter = rows // 2
    one, two, three = slice(0, rows), slice(rows, 2 * rows), slice(2 * rows, 3 * rows)
    base, tail = slice(rows, rows + quarter), rows + quarter
    corner = total[three, three]
    top, bottom = corner[:quarter], pltpu.roll(corner[quarter:], quarter, 1)
    mixed = jnp.where(i_at <= j_at, total[one, one], total[two, two])
    everyone[0, one, one] = total[one, two]
    everyone[0, one, two] = total[one, three]
    everyone[0, one, three] = total[two, three]
    everyone[0, base, one] = mixed[:quarter]
    everyone[0, base, two] = mixed[quarter:]
    everyone[0, base, three] = jnp.where((i_at <= j_at)[:quarter], top, bottom)
    everyone[0, tail:] = jnp.zeros((8, size), jnp.float32)
    everyone[0, tail : tail + 2, :slots] = send[0].astype(jnp.float32)
    everyone[0, tail : tail + 1, two] = jnp.sum(
        jnp.where(i_at == j_at, total[two, two], 0.0), axis=0, keepdims=True)
    everyone[0, tail : tail + 1, three] = jnp.sum(jnp.where(i_at == j_at, corner, 0.0), axis=0, keepdims=True)

    def m_copy(h, dom, to, k):
        return pltpu.make_async_remote_copy(
            src_ref=everyone.at[seat_of(dom, me), pl.ds(*HALVES[h])],
            dst_ref=everyone.at[seat_of(dom, to), pl.ds(*HALVES[h])], send_sem=m_send.at[h, k],
            recv_sem=m_recv.at[h, seat_of(dom, to)], device_id={"dom": to}, device_id_type=MESH)

    def m_wait(h, dom):
        part = everyone.at[seat_of(dom, me), pl.ds(*HALVES[h])]
        pltpu.make_async_remote_copy(
            src_ref=part, dst_ref=part, send_sem=m_send.at[h, 0], recv_sem=m_recv.at[h, seat_of(dom, me)],
            device_id={"dom": sib}, device_id_type=MESH).wait_recv()

    def y_copy(c, dom, to, k):
        return pltpu.make_async_remote_copy(
            src_ref=gathered.at[seat_of(dom, me), rows_of(c)], dst_ref=gathered.at[seat_of(dom, to), rows_of(c)],
            send_sem=y_send.at[c, k], recv_sem=y_recv.at[c, seat_of(dom, to)], device_id={"dom": to},
            device_id_type=MESH)

    def y_wait(c, dom):
        part = gathered.at[seat_of(dom, me), rows_of(c)]
        pltpu.make_async_remote_copy(
            src_ref=part, dst_ref=part, send_sem=y_send.at[c, 0], recv_sem=y_recv.at[c, seat_of(dom, me)],
            device_id={"dom": sib}, device_id_type=MESH).wait_recv()

    unsent = []

    def go(copy):
        copy.start()
        unsent.append(copy)

    def first_hop(copy):
        go(copy(me, x_next, 0))
        go(copy(me, y_next, 1))
        go(copy(me, sib, 2))

    def second_hop(copy, wait):
        wait(x_next)
        wait(y_next)
        go(copy(across, onward, 3))
        go(copy(x_next, sib, 4))
        go(copy(y_next, sib, 5))

    def third_hop(copy, wait):
        wait(diag)
        go(copy(diag, sib, 6))

    away = [sib, x_next + 1 - 2 * core, y_next + 1 - 2 * core, diag + 1 - 2 * core]

    copies = [functools.partial(m_copy, h) for h in range(2)]
    waits = [functools.partial(m_wait, h) for h in range(2)]
    for h in range(2):
        first_hop(copies[h])

    for copy in loads[4:]:
        copy.wait()
    partial(2)
    partial(1)
    send_right(ORDER[2:])
    send_left(ORDER[2:])

    def relay(k):
        def right(j, c):
            to_right(j, c).wait_recv()
            acc[j, rows_of(c)] = acc[j, rows_of(c)] + from_left[j, rows_of(c)]
            to_right(j, c).start()

        def left(j, c):
            to_left(j, c).wait_recv()
            acc[j, rows_of(c)] = acc[j, rows_of(c)] + from_right[j, rows_of(c)]
            to_left(j, c).start()

        last = bands - 1
        for hop in (1, 2):
            at = k - hop + 1
            if not 0 <= at < len(ORDER):
                continue
            j, c = ORDER[at]
            if j > hop:
                @pl.when(z == hop)
                def _():
                    right(j, c)

                @pl.when(z == last - hop)
                def _():
                    left(last - j, c)

    def finish(c):
        part = rows_of(c)
        gathered[0, part] = acc[z, part]

        @pl.when(z > 0)
        def _():
            to_right(z, c).wait_recv()
            gathered[0, part] = gathered[0, part] + from_left[z, part]

        @pl.when(z < bands - 1)
        def _():
            to_left(z, c).wait_recv()
            gathered[0, part] = gathered[0, part] + from_right[z, part]

        first_hop(functools.partial(y_copy, c))

    def y_second(c):
        second_hop(functools.partial(y_copy, c), functools.partial(y_wait, c))

    def y_third(c):
        third_hop(functools.partial(y_copy, c), functools.partial(y_wait, c))

    def y_split(c):
        for dom in away:
            y_wait(c, dom)
        first, count = SPAN[c]
        for d in range(doms):
            high, low = high_low(gathered[d, first : first + count])
            at = doms * first + d * count
            y_high[at : at + count] = high
            y_low[at : at + count] = low

    def prepare(d):
        straight = jnp.concatenate([everyone[d, base, one], everyone[d, base, two]], axis=0)
        across_it = jnp.transpose(straight)
        piece = everyone[d, base, three]
        folded = jnp.concatenate([piece, pltpu.roll(piece, quarter, 1)], axis=0)
        unfolded = jnp.transpose(folded)
        second_line, third_line = everyone[d, tail : tail + 1, two], everyone[d, tail : tail + 1, three]
        first_block = jnp.where(i_at <= j_at, straight, across_it)
        second_block = jnp.where(i_at > j_at, straight, jnp.where(i_at < j_at, across_it, second_line))
        direct = ((i_at < quarter) & (i_at <= j_at)) | ((j_at >= quarter) & (i_at > j_at))
        third_block = jnp.where(
            direct, folded, jnp.where((i_at == j_at) & (i_at >= quarter), third_line, unfolded))
        ab, ac, bc = everyone[d, one, one], everyone[d, one, two], everyone[d, one, three]
        lines = (
            (one, (first_block, ab, ac)),
            (two, (jnp.transpose(ab), second_block, bc)),
            (three, (jnp.transpose(ac), jnp.transpose(bc), third_block)),
        )
        for line, blocks in lines:
            m_high, m_low = high_low(jnp.concatenate(blocks, axis=1))
            matrix[d, line, :size] = m_high
            matrix[d, line, size : 2 * size] = m_low
            matrix[d, line, 2 * size :] = m_high
        tile = everyone[d, tail:, :LANES]
        other = pltpu.roll(tile, slots, 1)
        first_lanes = lax.broadcasted_iota(jnp.int32, (1, LANES), 1) < slots
        row = jnp.where(first_lanes, tile[0:1], other[1:2]).astype(jnp.int32)
        at = lax.broadcasted_iota(jnp.int32, (owned, LANES), 0)
        hot = jnp.where(at == row, 1.0, 0.0)
        spread[d, :, :LANES] = hot.astype(b16)
        spread[d, :, LANES:] = hot.astype(b16)
        pick[d] = jnp.transpose(hot).astype(b16)

    pieces[...] = jnp.zeros_like(pieces)
    ghosts[...] = jnp.zeros_like(ghosts)
    eye = jnp.where(
        lax.broadcasted_iota(jnp.int32, (owned, owned), 0) == lax.broadcasted_iota(jnp.int32, (owned, owned), 1),
        1.0, 0.0)
    even[0] = eye
    pieces[0, :owned] = eye.astype(b16)
    pieces[0, size : size + owned] = eye.astype(b16)
    prepare(0)

    def ready(dom):
        prepare(seat_of(dom, me))

    for wait in waits:
        wait(sib)
    ready(sib)
    relay(0)
    second_hop(copies[0], waits[0])
    relay(1)
    second_hop(copies[1], waits[1])
    ready(x_next)
    ready(y_next)
    third_hop(copies[0], waits[0])
    relay(2)
    for dom in away[1:3]:
        for wait in waits:
            wait(dom)
        ready(dom)
    third_hop(copies[1], waits[1])
    ready(diag)
    relay(3)
    for wait in waits:
        wait(away[3])
    ready(away[3])
    finish(0)

    every = list(range(doms))
    held = [[0], [6, 7, 0, 1, 2]]
    busy = [[7, 0, 1], [5, 6, 7, 0, 1, 2, 3]]

    def advance(k, middle=()):
        end = k == DEGREE
        source = held[k - 1] if k <= 2 else every
        active = busy[k - 1] if k <= 2 else every
        result = held[k] if k < 2 else every
        old = [] if k == 1 else held[k - 2] if k <= 3 else every
        store = odd if k % 2 else even
        for d in source:
            after, ahead = (d + 1) % doms, (d - 1) % doms
            for at, bases in ((0, (0, size)), (2 * size, (2 * size,))):
                g = mm(pick[d], pieces[d, at : at + owned]).astype(b16)
                for base in bases:
                    pieces[after, base + owned : base + owned + slots] = g[:slots]
                    pieces[ahead, base + owned + slots : base + size] = g[slots:]
        for d in active:
            after, ahead = (d + 1) % doms, (d - 1) % doms
            y = mm(matrix[d], pieces[d])
            image[d] = y[:owned]
            high, low = high_low(y[owned:])
            ghosts[ahead, :slots] = high[:slots]
            ghosts[ahead, 2 * slots : 3 * slots] = low[:slots]
            ghosts[after, slots : 2 * slots] = high[slots:]
            ghosts[after, 3 * slots :] = low[slots:]
        for act, c in middle:
            act(c)
        for d in result:
            y = mm(spread[d], ghosts[d])
            if d in active:
                y = y + image[d]
            v = y if k == 1 else 2.0 * y
            if d in old:
                v = v - store[d]
            if end:
                for first, count in SPAN:
                    at = doms * first + d * count
                    odd[at // owned, at % owned : at % owned + count] = v[first : first + count]
            else:
                store[d] = v
                high, low = high_low(v)
                pieces[d, :owned] = high
                pieces[d, size : size + owned] = high
                pieces[d, 2 * size : 2 * size + owned] = low

    advance(1)
    advance(2, [(relay, 4)])
    y_second(0)
    advance(3, [(relay, 5)])
    y_third(0)
    advance(4, [(relay, 6)])
    relay(7)
    finish(1)
    advance(5, [(relay, 8)])
    y_split(0)
    advance(6, [(relay, 9), (y_second, 1)])
    relay(10)
    finish(2)
    advance(7, [(relay, 11), (y_third, 1)])
    relay(12)
    advance(8, [(y_second, 2), (relay, 13), (finish, 3)])
    relay(14)
    finish(4)
    y_third(2)
    y_split(1)
    y_second(3)
    for d in range(doms):
        high, low = high_low(jnp.transpose(odd[d]))
        p_high[:, d * owned : (d + 1) * owned] = high
        p_low[:, d * owned : (d + 1) * owned] = low
    y_second(4)
    y_split(2)
    y_third(3)
    y_third(4)
    y_split(3)

    def product(at):
        high, low = y_high[at], y_low[at]
        return mm(p_high[:, at], high) + (mm(p_high[:, at], low) + mm(p_low[:, at], high))

    bulk = doms * SPAN[-1][0]
    out[...] = product(slice(0, bulk))
    y_split(4)
    out[...] = out[...] + product(slice(bulk, doms * owned))

    for copy in unsent:
        copy.wait_send()
    for j in range(bands):
        for c in range(len(SPAN)):
            @pl.when(z < j)
            def _():
                to_right(j, c).wait_send()

            @pl.when(z > j)
            def _():
                to_left(j, c).wait_send()


def fused(waves, cell_matrix, connect, send_index, rotation):
    owned, width = waves.shape
    slots = send_index.shape[2]
    bands = lax.axis_size("band")
    size = owned + 2 * slots
    doms = 8
    vmem = pl.BlockSpec(memory_space=pltpu.VMEM)
    anywhere = pl.BlockSpec(memory_space=pl.ANY)
    cells = jnp.swapaxes(cell_matrix, 0, 1)
    f32, b16 = jnp.float32, jnp.bfloat16
    dma = pltpu.SemaphoreType.DMA
    return pl.pallas_call(
        functools.partial(fused_kernel, bands, owned, slots),
        out_shape=jax.ShapeDtypeStruct((owned, width), f32),
        in_specs=[anywhere, anywhere, vmem, vmem, anywhere],
        out_specs=vmem,
        scratch_shapes=[
            pltpu.VMEM((owned, width), f32),
            pltpu.VMEM(cells.shape, f32),
            pltpu.VMEM(rotation.shape, f32),
            dma((bands + 2,)),
            pltpu.VMEM((bands, owned, width), f32),
            pltpu.VMEM((bands, owned, width), f32),
            pltpu.VMEM((bands, owned, width), f32),
            pltpu.VMEM((doms, HALVES[1][0] + HALVES[1][1], size), f32),
            pltpu.VMEM((doms, size, 3 * size), b16),
            pltpu.VMEM((doms, 2 * slots, owned), b16),
            pltpu.VMEM((doms, owned, 4 * slots), b16),
            pltpu.VMEM((doms, 3 * size, owned), b16),
            pltpu.VMEM((doms, 4 * slots, owned), b16),
            pltpu.VMEM((doms, owned, owned), f32),
            pltpu.VMEM((doms, owned, owned), f32),
            pltpu.VMEM((doms, owned, owned), f32),
            pltpu.VMEM((doms, owned, width), f32),
            pltpu.VMEM((doms * owned, width), b16),
            pltpu.VMEM((doms * owned, width), b16),
            pltpu.VMEM((owned, doms * owned), b16),
            pltpu.VMEM((owned, doms * owned), b16),
            dma((bands, len(SPAN))), dma((bands, len(SPAN))), dma((bands, len(SPAN))),
            dma((2, 7)), dma((2, doms)),
            dma((len(SPAN), 7)), dma((len(SPAN), doms)),
        ],
        compiler_params=pltpu.CompilerParams(
            vmem_limit_bytes=60 * 2**20, collective_id=0, has_side_effects=True),
        cost_estimate=pl.CostEstimate(
            flops=DEGREE * doms * 6 * size * size * owned, bytes_accessed=2**24, transcendentals=0),
    )(waves, cells, connect, send_index, rotation)


def shards(waves, cell_matrix, connect, send_index, rotation):
    owned = waves.shape[0]
    width = waves.shape[1]
    slots = send_index.shape[2]
    doms = lax.axis_size("dom")
    if doms == 8 and width == doms * LANES // 2 and 2 * slots == LANES and owned == 2 * LANES and lax.axis_size("band") == 4:
        return fused(waves, cell_matrix, connect, send_index, rotation)
    size = owned + 2 * slots
    seat = jax.nn.one_hot(connect, size, dtype=jnp.float32)
    half_way = jnp.einsum("cij,cjn->cin", cell_matrix, seat, precision=lax.Precision.HIGH)
    local = jnp.einsum("cim,cin->mn", seat, half_way, precision=lax.Precision.HIGH)
    node = jnp.arange(size)
    shift = jnp.where((node[:, None] == node[None, :]) & (node[:, None] < owned), centre, 0.0)
    local = (local - shift) / half_width
    row = jnp.zeros((8, size), jnp.float32).at[0, : 2 * slots].set(
        send_index.reshape(-1).astype(jnp.float32)
    )
    everyone = lax.all_gather(jnp.concatenate([local, row], axis=0), "dom")
    high, low = split(everyone[:, :size])
    index = everyone[:, size, : 2 * slots].astype(jnp.int32)
    pick = jax.nn.one_hot(index, owned, dtype=jnp.bfloat16)
    spread = jnp.swapaxes(pick, 1, 2)

    partial = jnp.dot(waves, rotation, precision=lax.Precision.HIGH, preferred_element_type=jnp.float32)
    turned = lax.psum_scatter(partial, "band", scatter_dimension=1, tiled=True)
    share = width // doms
    columns = lax.all_to_all(turned, "dom", split_axis=1, concat_axis=0, tiled=True)
    columns = columns.reshape(doms, owned, share)
    half = LANES // 2
    columns = jnp.pad(columns, ((0, 0), (0, 0), (0, half - share)))
    columns = jnp.concatenate([columns, columns], axis=2)
    vmem = pl.BlockSpec(memory_space=pltpu.VMEM)
    done = pl.pallas_call(
        functools.partial(filter_kernel, doms, owned, slots, half),
        out_shape=jax.ShapeDtypeStruct((doms, owned, LANES), jnp.float32),
        in_specs=[vmem] * 5,
        out_specs=vmem,
        scratch_shapes=[
            pltpu.VMEM((doms, size, LANES), jnp.bfloat16),
            pltpu.VMEM((doms, 2 * slots, LANES), jnp.bfloat16),
            pltpu.VMEM((doms, owned, LANES), jnp.float32),
            pltpu.VMEM((doms, owned, LANES), jnp.float32),
        ],
        compiler_params=pltpu.CompilerParams(vmem_limit_bytes=56 * 2**20),
        cost_estimate=pl.CostEstimate(
            flops=DEGREE * doms * 4 * size * size * LANES, bytes_accessed=2**24, transcendentals=0
        ),
    )(high, low, pick, spread, columns)
    back = done[:, :, :share].reshape(doms * owned, share)
    return lax.all_to_all(back, "dom", split_axis=0, concat_axis=1, tiled=True)


def solution(mesh):
    in_specs = (
        P("dom", "band"),
        P("dom", None, None),
        P("dom", None),
        P("dom", None, None),
        P("band", None),
    )
    out_specs = P("dom", "band")
    return jax.shard_map(shards, mesh=mesh, in_specs=in_specs, out_specs=out_specs, check_vma=False)
```

```python
import functools

import jax
import jax.numpy as jnp
from jax import lax
from jax.experimental import pallas as pl
from jax.experimental.pallas import tpu as pltpu
from jax.sharding import PartitionSpec as P

DEGREE = 8
LANES = 128
MESH = pl.DeviceIdType.MESH
SPAN = ((0, 96), (96, 64), (160, 48), (208, 32), (240, 16))
ORDER = ((3, 0), (2, 0), (3, 1), (1, 0), (3, 2), (2, 1), (1, 1), (3, 3), (2, 2), (1, 2), (3, 4), (2, 3), (2, 4),
         (1, 3), (1, 4))
FIRST, LINK, HOP, STOP, READY = 4.2, 2.8 / 64, 1.7, 0.2, 22.0
STOPS = (3, 7)
HALVES = ((0, 104), (104, 96))


centre = 5.5
half_width = 9.5


def split(x):
    high = lax.reduce_precision(x, 8, 7)
    return high.astype(jnp.bfloat16), (x - high).astype(jnp.bfloat16)


def doubled(x, half):
    return x + pltpu.roll(x, half, 1)


def packed(x, half):
    high = x.astype(jnp.bfloat16)
    low = (x - high.astype(jnp.float32)).astype(jnp.bfloat16)
    lane = lax.broadcasted_iota(jnp.int32, x.shape, 1)
    return jnp.where(lane < half, high.astype(jnp.float32), low.astype(jnp.float32)).astype(
        jnp.bfloat16
    )


def mm(a, b):
    return jnp.dot(a, b, preferred_element_type=jnp.float32)


def filter_kernel(doms, owned, slots, half, high, low, pick, spread, start, out, pieces, ghosts, before, image):
    unroll = doms <= 8

    def over(body):
        if unroll:
            for d in range(doms):
                body(d)
        else:
            pl.loop(0, doms)(body)

    def begin(d):
        v = start[d]
        out[d] = v
        before[d] = jnp.zeros_like(v)
        pieces[d, :owned] = packed(v, half)

    over(begin)

    def one(step, _):
        def send(d):
            after = lax.rem(d + 1, doms) if not unroll else (d + 1) % doms
            ahead = lax.rem(d + doms - 1, doms) if not unroll else (d - 1) % doms
            g = mm(pick[d], pieces[d, :owned]).astype(jnp.bfloat16)
            pieces[after, owned : owned + slots] = g[:slots]
            pieces[ahead, owned + slots :] = g[slots:]

        over(send)

        def apply(d):
            x = pieces[d]
            y = mm(high[d], x) + mm(low[d], x)
            y = doubled(y, half)
            image[d] = y[:owned]
            after = lax.rem(d + 1, doms) if not unroll else (d + 1) % doms
            ahead = lax.rem(d + doms - 1, doms) if not unroll else (d - 1) % doms
            r = packed(y[owned:], half)
            ghosts[ahead, :slots] = r[:slots]
            ghosts[after, slots:] = r[slots:]

        over(apply)
        scale = jnp.where(step == 0, 1.0, 2.0)

        def update(d):
            y = image[d] + doubled(mm(spread[d], ghosts[d]), half)
            v = scale * y - before[d]
            before[d] = out[d]
            out[d] = v
            pieces[d, :owned] = packed(v, half)

        over(update)
        return 0

    lax.fori_loop(0, DEGREE, one, 0)


def high_low(x):
    high = x.astype(jnp.bfloat16)
    return high, (x - high.astype(jnp.float32)).astype(jnp.bfloat16)


def fused_kernel(bands, owned, slots, waves_in, cells_in, conn, send, rotation_in, out, *scratch):
    (waves, cells, rotation, load, acc, from_left, from_right, everyone, matrix, pick, spread, pieces, ghosts, image, even, odd,
     gathered, y_high, y_low, p_high, p_low,
     z_send, z_right, z_left, m_send, m_recv, y_send, y_recv) = scratch
    doms = 8
    size = owned + 2 * slots
    rows = owned // 2
    b16 = jnp.bfloat16
    me = lax.axis_index("dom")
    z = lax.axis_index("band")
    core = lax.rem(me, 2)
    place = lax.rem(lax.div(me, 2), 2)
    upper = lax.div(me, 4)
    sib = me + 1 - 2 * core
    x_next = me + 2 - 4 * place
    y_next = me + 4 - 8 * upper
    diag = x_next + 4 - 8 * upper
    across = x_next * (1 - core) + y_next * core
    onward = y_next * (1 - core) + x_next * core

    def seat_of(dom, at):
        return lax.rem(dom - at + doms, doms)

    barrier = pltpu.get_barrier_semaphore()
    for t in range(1, doms):
        pl.semaphore_signal(barrier, inc=1, device_id={"dom": lax.rem(me + t, doms)}, device_id_type=MESH)

    @pl.when(z > 0)
    def _():
        pl.semaphore_signal(barrier, inc=1, device_id={"band": z - 1}, device_id_type=MESH)

    @pl.when(z < bands - 1)
    def _():
        pl.semaphore_signal(barrier, inc=1, device_id={"band": z + 1}, device_id_type=MESH)

    width = waves.shape[1]

    def block(j):
        return pl.ds(j * width, width)

    order = []
    for r in range(bands // 2):
        order += [bands - 1 - r, r]
    loads = [pltpu.make_async_copy(waves_in, waves, load.at[bands + 1])]
    loads += [pltpu.make_async_copy(rotation_in.at[:, block(j)], rotation.at[:, block(j)], load.at[j]) for j in order]
    loads.insert(3, pltpu.make_async_copy(cells_in, cells, load.at[bands]))
    for copy in loads:
        copy.start()

    def rows_of(c):
        return pl.ds(*SPAN[c])

    def to_right(j, c):
        return pltpu.make_async_remote_copy(
            src_ref=acc.at[j, rows_of(c)], dst_ref=from_left.at[j, rows_of(c)], send_sem=z_send.at[j, c],
            recv_sem=z_right.at[j, c], device_id={"band": z + 1}, device_id_type=MESH)

    def to_left(j, c):
        return pltpu.make_async_remote_copy(
            src_ref=acc.at[j, rows_of(c)], dst_ref=from_right.at[j, rows_of(c)], send_sem=z_send.at[j, c],
            recv_sem=z_left.at[j, c], device_id={"band": z - 1}, device_id_type=MESH)

    def send_right(items):
        @pl.when(z == 0)
        def _():
            for j, c in items:
                to_right(j, c).start()

    def send_left(items):
        @pl.when(z == bands - 1)
        def _():
            for j, c in items:
                to_left(bands - 1 - j, c).start()

    loads[0].wait()
    w_high, w_low = high_low(waves[...])

    def partial(j):
        r_high, r_low = high_low(rotation[:, j * width : (j + 1) * width])
        acc[j] = mm(w_high, r_high) + (mm(w_high, r_low) + mm(w_low, r_high))

    loads[1].wait()
    partial(3)
    loads[2].wait()
    partial(0)
    beside = lax.div(z + bands - 1, bands) + lax.div(2 * bands - 2 - z, bands)
    pl.semaphore_wait(barrier, doms - 1 + beside)

    send_right(ORDER[:1])
    send_left(ORDER[:1])

    loads[3].wait()
    node = lax.broadcasted_iota(jnp.int32, (size, conn.shape[1]), 0)
    total = jnp.zeros((size, size), jnp.float32)
    for c in range(cells.shape[1]):
        seat = jnp.where(node == conn[c : c + 1, :], 1.0, 0.0).astype(b16)
        a_high, a_low = high_low(cells[:, c, :])
        b_high, b_low = high_low(mm(seat, a_high) + mm(seat, a_low))
        dims = (((1,), (1,)), ((), ()))
        total = total + (
            lax.dot_general(b_high, seat, dims, preferred_element_type=jnp.float32)
            + lax.dot_general(b_low, seat, dims, preferred_element_type=jnp.float32))
    r_at = lax.broadcasted_iota(jnp.int32, (size, size), 0)
    c_at = lax.broadcasted_iota(jnp.int32, (size, size), 1)
    shift = jnp.where((r_at == c_at) & (r_at < owned), centre, 0.0)
    total = (total - shift) / half_width
    i_at = lax.broadcasted_iota(jnp.int32, (rows, rows), 0)
    j_at = lax.broadcasted_iota(jnp.int32, (rows, rows), 1)
    quarter = rows // 2
    one, two, three = slice(0, rows), slice(rows, 2 * rows), slice(2 * rows, 3 * rows)
    base, tail = slice(rows, rows + quarter), rows + quarter
    corner = total[three, three]
    top, bottom = corner[:quarter], pltpu.roll(corner[quarter:], quarter, 1)
    mixed = jnp.where(i_at <= j_at, total[one, one], total[two, two])
    everyone[0, one, one] = total[one, two]
    everyone[0, one, two] = total[one, three]
    everyone[0, one, three] = total[two, three]
    everyone[0, base, one] = mixed[:quarter]
    everyone[0, base, two] = mixed[quarter:]
    everyone[0, base, three] = jnp.where((i_at <= j_at)[:quarter], top, bottom)
    everyone[0, tail:] = jnp.zeros((8, size), jnp.float32)
    everyone[0, tail : tail + 2, :slots] = send[0].astype(jnp.float32)
    everyone[0, tail : tail + 1, two] = jnp.sum(
        jnp.where(i_at == j_at, total[two, two], 0.0), axis=0, keepdims=True)
    everyone[0, tail : tail + 1, three] = jnp.sum(jnp.where(i_at == j_at, corner, 0.0), axis=0, keepdims=True)

    def m_copy(h, dom, to, k):
        return pltpu.make_async_remote_copy(
            src_ref=everyone.at[seat_of(dom, me), pl.ds(*HALVES[h])],
            dst_ref=everyone.at[seat_of(dom, to), pl.ds(*HALVES[h])], send_sem=m_send.at[h, k],
            recv_sem=m_recv.at[h, seat_of(dom, to)], device_id={"dom": to}, device_id_type=MESH)

    def m_wait(h, dom):
        part = everyone.at[seat_of(dom, me), pl.ds(*HALVES[h])]
        pltpu.make_async_remote_copy(
            src_ref=part, dst_ref=part, send_sem=m_send.at[h, 0], recv_sem=m_recv.at[h, seat_of(dom, me)],
            device_id={"dom": sib}, device_id_type=MESH).wait_recv()

    def y_copy(c, dom, to, k):
        return pltpu.make_async_remote_copy(
            src_ref=gathered.at[seat_of(dom, me), rows_of(c)], dst_ref=gathered.at[seat_of(dom, to), rows_of(c)],
            send_sem=y_send.at[c, k], recv_sem=y_recv.at[c, seat_of(dom, to)], device_id={"dom": to},
            device_id_type=MESH)

    def y_wait(c, dom):
        part = gathered.at[seat_of(dom, me), rows_of(c)]
        pltpu.make_async_remote_copy(
            src_ref=part, dst_ref=part, send_sem=y_send.at[c, 0], recv_sem=y_recv.at[c, seat_of(dom, me)],
            device_id={"dom": sib}, device_id_type=MESH).wait_recv()

    unsent = []

    def go(copy):
        copy.start()
        unsent.append(copy)

    def first_hop(copy):
        go(copy(me, x_next, 0))
        go(copy(me, y_next, 1))
        go(copy(me, sib, 2))

    def second_hop(copy, wait):
        wait(x_next)
        wait(y_next)
        go(copy(across, onward, 3))
        go(copy(x_next, sib, 4))
        go(copy(y_next, sib, 5))

    def third_hop(copy, wait):
        wait(diag)
        go(copy(diag, sib, 6))

    away = [sib, x_next + 1 - 2 * core, y_next + 1 - 2 * core, diag + 1 - 2 * core]

    copies = [functools.partial(m_copy, h) for h in range(2)]
    waits = [functools.partial(m_wait, h) for h in range(2)]
    for h in range(2):
        first_hop(copies[h])

    for copy in loads[4:]:
        copy.wait()
    partial(2)
    partial(1)
    send_right(ORDER[1:])
    send_left(ORDER[1:])

    def relay(k, hop):
        def right(j, c):
            to_right(j, c).wait_recv()
            acc[j, rows_of(c)] = acc[j, rows_of(c)] + from_left[j, rows_of(c)]
            to_right(j, c).start()

        def left(j, c):
            to_left(j, c).wait_recv()
            acc[j, rows_of(c)] = acc[j, rows_of(c)] + from_right[j, rows_of(c)]
            to_left(j, c).start()

        last = bands - 1
        j, c = ORDER[k]

        @pl.when(z == hop)
        def _():
            right(j, c)

        @pl.when(z == last - hop)
        def _():
            left(last - j, c)

    def finish(c):
        part = rows_of(c)
        gathered[0, part] = acc[z, part]

        @pl.when(z > 0)
        def _():
            to_right(z, c).wait_recv()
            gathered[0, part] = gathered[0, part] + from_left[z, part]

        @pl.when(z < bands - 1)
        def _():
            to_left(z, c).wait_recv()
            gathered[0, part] = gathered[0, part] + from_right[z, part]

        if c == len(SPAN) - 1:
            for k, dom in enumerate((diag, away[3], x_next, y_next, away[1], away[2], sib)):
                go(y_copy(c, me, dom, k))
        else:
            for k, dom in enumerate((diag, x_next, y_next, sib)):
                go(y_copy(c, me, dom, k))

    def pass_on(c):
        for k, dom in enumerate((x_next, y_next, diag)):
            y_wait(c, dom)
            go(y_copy(c, dom, sib, 4 + k))

    def y_split(c):
        others = (x_next, y_next, diag) if c == len(SPAN) - 1 else ()
        for dom in (*away, *others):
            y_wait(c, dom)
        first, count = SPAN[c]
        for d in range(doms):
            high, low = high_low(gathered[d, first : first + count])
            at = doms * first + d * count
            y_high[at : at + count] = high
            y_low[at : at + count] = low

    def prepare(d):
        straight = jnp.concatenate([everyone[d, base, one], everyone[d, base, two]], axis=0)
        across_it = jnp.transpose(straight)
        piece = everyone[d, base, three]
        folded = jnp.concatenate([piece, pltpu.roll(piece, quarter, 1)], axis=0)
        unfolded = jnp.transpose(folded)
        second_line, third_line = everyone[d, tail : tail + 1, two], everyone[d, tail : tail + 1, three]
        first_block = jnp.where(i_at <= j_at, straight, across_it)
        second_block = jnp.where(i_at > j_at, straight, jnp.where(i_at < j_at, across_it, second_line))
        direct = ((i_at < quarter) & (i_at <= j_at)) | ((j_at >= quarter) & (i_at > j_at))
        third_block = jnp.where(
            direct, folded, jnp.where((i_at == j_at) & (i_at >= quarter), third_line, unfolded))
        ab, ac, bc = everyone[d, one, one], everyone[d, one, two], everyone[d, one, three]
        lines = (
            (one, (first_block, ab, ac)),
            (two, (jnp.transpose(ab), second_block, bc)),
            (three, (jnp.transpose(ac), jnp.transpose(bc), third_block)),
        )
        for line, blocks in lines:
            m_high, m_low = high_low(jnp.concatenate(blocks, axis=1))
            matrix[d, line, :size] = m_high
            matrix[d, line, size : 2 * size] = m_low
            matrix[d, line, 2 * size :] = m_high
        tile = everyone[d, tail:, :LANES]
        other = pltpu.roll(tile, slots, 1)
        first_lanes = lax.broadcasted_iota(jnp.int32, (1, LANES), 1) < slots
        row = jnp.where(first_lanes, tile[0:1], other[1:2]).astype(jnp.int32)
        at = lax.broadcasted_iota(jnp.int32, (owned, LANES), 0)
        hot = jnp.where(at == row, 1.0, 0.0)
        spread[d, :, :LANES] = hot.astype(b16)
        spread[d, :, LANES:] = hot.astype(b16)
        pick[d] = jnp.transpose(hot).astype(b16)

    agenda, late = [], []
    arrival, clock = {}, FIRST
    for k, (j, c) in enumerate(ORDER):
        clock += LINK * SPAN[c][1]
        arrival[j, c, 1] = clock
        for hop in range(1, j):
            agenda.append((arrival[j, c, hop] + STOP, relay, (k, hop)))
            arrival[j, c, hop + 1] = arrival[j, c, hop] + STOP + LINK * SPAN[c][1] + HOP
    for c, (first, count) in enumerate(SPAN):
        done = max(arrival[1, c, 1], arrival[2, c, 2], arrival[3, c, 3]) + 2 * STOP
        agenda.append((done, finish, (c,)))
        done += 2 * LINK * count + HOP + 1.0
        if c < len(SPAN) - 1:
            agenda.append((done, pass_on, (c,)))
        agenda.append((done + 2.0, y_split, (c,)))
        if c >= len(SPAN) - 3:
            late.append(agenda.pop())
            if c == len(SPAN) - 2:
                late.insert(0, agenda.pop())
    agenda.sort(key=lambda item: item[0])

    def tick(now):
        while agenda and agenda[0][0] <= now:
            _, act, details = agenda.pop(0)
            act(*details)

    pieces[...] = jnp.zeros_like(pieces)
    ghosts[...] = jnp.zeros_like(ghosts)
    eye = jnp.where(
        lax.broadcasted_iota(jnp.int32, (owned, owned), 0) == lax.broadcasted_iota(jnp.int32, (owned, owned), 1),
        1.0, 0.0)
    even[:owned] = eye
    pieces[0, :owned] = eye.astype(b16)
    pieces[0, size : size + owned] = eye.astype(b16)
    prepare(0)

    def ready(dom):
        prepare(seat_of(dom, me))

    for wait in waits:
        wait(sib)
    ready(sib)
    tick(READY - 11.0)
    second_hop(copies[0], waits[0])
    tick(READY - 9.0)
    second_hop(copies[1], waits[1])
    ready(x_next)
    ready(y_next)
    tick(READY - 6.0)
    third_hop(copies[0], waits[0])
    for dom in away[1:3]:
        for wait in waits:
            wait(dom)
        ready(dom)
    third_hop(copies[1], waits[1])
    ready(diag)
    tick(READY - 2.0)
    for wait in waits:
        wait(away[3])
    ready(away[3])

    every = list(range(doms))
    held = [[0], [6, 7, 0, 1, 2]]
    busy = [[7, 0, 1], [5, 6, 7, 0, 1, 2, 3]]

    now = [READY]

    def spend(time):
        now[0] += time

    def advance(k):
        end = k == DEGREE
        source = held[k - 1] if k <= 2 else every
        active = busy[k - 1] if k <= 2 else every
        result = held[k] if k < 2 else every
        old = [] if k == 1 else held[k - 2] if k <= 3 else every
        store = odd if k % 2 else even
        for d in source:
            after, ahead = (d + 1) % doms, (d - 1) % doms
            for at, bases in ((0, (0, size)), (2 * size, (2 * size,))):
                g = mm(pick[d], pieces[d, at : at + owned]).astype(b16)
                for base in bases:
                    pieces[after, base + owned : base + owned + slots] = g[:slots]
                    pieces[ahead, base + owned + slots : base + size] = g[slots:]
        spend(0.05 * len(source))
        for d in active:
            after, ahead = (d + 1) % doms, (d - 1) % doms
            y = mm(matrix[d], pieces[d])
            image[d] = y[:owned]
            high, low = high_low(y[owned:])
            ghosts[ahead, :slots] = high[:slots]
            ghosts[ahead, 2 * slots : 3 * slots] = low[:slots]
            ghosts[after, slots : 2 * slots] = high[slots:]
            ghosts[after, 3 * slots :] = low[slots:]
            spend(0.28)
            if d in STOPS:
                tick(now[0])
        for d in result:
            home = slice(d * owned, (d + 1) * owned)
            y = mm(spread[d], ghosts[d])
            if d in active:
                y = y + image[d]
            v = y if k == 1 else 2.0 * y
            if d in old:
                v = v - store[home]
            if end:
                for first, count in SPAN:
                    at = doms * first + d * count
                    odd[at : at + count] = v[first : first + count]
            else:
                store[home] = v
                high, low = high_low(v)
                pieces[d, :owned] = high
                pieces[d, size : size + owned] = high
                pieces[d, 2 * size : 2 * size + owned] = low
        spend(0.055 * len(result))

    for k in range(1, DEGREE + 1):
        advance(k)
    tick(1000.0)
    for d in range(doms):
        high, low = high_low(jnp.transpose(odd[d * owned : (d + 1) * owned]))
        p_high[:, d * owned : (d + 1) * owned] = high
        p_low[:, d * owned : (d + 1) * owned] = low

    def product(at):
        high, low = y_high[at], y_low[at]
        return mm(p_high[:, at], high) + (mm(p_high[:, at], low) + mm(p_low[:, at], high))

    bulk = doms * SPAN[-2][0]
    for _, act, details in late[:2]:
        act(*details)
    out[...] = product(slice(0, bulk))
    for _, act, details in late[2:]:
        act(*details)
    out[...] = out[...] + product(slice(bulk, doms * owned))

    for copy in unsent:
        copy.wait_send()
    for j in range(bands):
        for c in range(len(SPAN)):
            @pl.when(z < j)
            def _():
                to_right(j, c).wait_send()

            @pl.when(z > j)
            def _():
                to_left(j, c).wait_send()


def fused(waves, cell_matrix, connect, send_index, rotation):
    owned, width = waves.shape
    slots = send_index.shape[2]
    bands = lax.axis_size("band")
    size = owned + 2 * slots
    doms = 8
    vmem = pl.BlockSpec(memory_space=pltpu.VMEM)
    anywhere = pl.BlockSpec(memory_space=pl.ANY)
    cells = jnp.swapaxes(cell_matrix, 0, 1)
    f32, b16 = jnp.float32, jnp.bfloat16
    dma = pltpu.SemaphoreType.DMA
    return pl.pallas_call(
        functools.partial(fused_kernel, bands, owned, slots),
        out_shape=jax.ShapeDtypeStruct((owned, width), f32),
        in_specs=[anywhere, anywhere, vmem, vmem, anywhere],
        out_specs=vmem,
        scratch_shapes=[
            pltpu.VMEM((owned, width), f32),
            pltpu.VMEM(cells.shape, f32),
            pltpu.VMEM(rotation.shape, f32),
            dma((bands + 2,)),
            pltpu.VMEM((bands, owned, width), f32),
            pltpu.VMEM((bands, owned, width), f32),
            pltpu.VMEM((bands, owned, width), f32),
            pltpu.VMEM((doms, HALVES[1][0] + HALVES[1][1], size), f32),
            pltpu.VMEM((doms, size, 3 * size), b16),
            pltpu.VMEM((doms, 2 * slots, owned), b16),
            pltpu.VMEM((doms, owned, 4 * slots), b16),
            pltpu.VMEM((doms, 3 * size, owned), b16),
            pltpu.VMEM((doms, 4 * slots, owned), b16),
            pltpu.VMEM((doms, owned, owned), f32),
            pltpu.VMEM((doms * owned, owned), f32),
            pltpu.VMEM((doms * owned, owned), f32),
            pltpu.VMEM((doms, owned, width), f32),
            pltpu.VMEM((doms * owned, width), b16),
            pltpu.VMEM((doms * owned, width), b16),
            pltpu.VMEM((owned, doms * owned), b16),
            pltpu.VMEM((owned, doms * owned), b16),
            dma((bands, len(SPAN))), dma((bands, len(SPAN))), dma((bands, len(SPAN))),
            dma((2, 7)), dma((2, doms)),
            dma((len(SPAN), 7)), dma((len(SPAN), doms)),
        ],
        compiler_params=pltpu.CompilerParams(
            vmem_limit_bytes=60 * 2**20, collective_id=0, has_side_effects=True),
        cost_estimate=pl.CostEstimate(
            flops=DEGREE * doms * 6 * size * size * owned, bytes_accessed=2**24, transcendentals=0),
    )(waves, cells, connect, send_index, rotation)


def shards(waves, cell_matrix, connect, send_index, rotation):
    owned = waves.shape[0]
    width = waves.shape[1]
    slots = send_index.shape[2]
    doms = lax.axis_size("dom")
    if doms == 8 and width == doms * LANES // 2 and 2 * slots == LANES and owned == 2 * LANES and lax.axis_size("band") == 4:
        return fused(waves, cell_matrix, connect, send_index, rotation)
    size = owned + 2 * slots
    seat = jax.nn.one_hot(connect, size, dtype=jnp.float32)
    half_way = jnp.einsum("cij,cjn->cin", cell_matrix, seat, precision=lax.Precision.HIGH)
    local = jnp.einsum("cim,cin->mn", seat, half_way, precision=lax.Precision.HIGH)
    node = jnp.arange(size)
    shift = jnp.where((node[:, None] == node[None, :]) & (node[:, None] < owned), centre, 0.0)
    local = (local - shift) / half_width
    row = jnp.zeros((8, size), jnp.float32).at[0, : 2 * slots].set(
        send_index.reshape(-1).astype(jnp.float32)
    )
    everyone = lax.all_gather(jnp.concatenate([local, row], axis=0), "dom")
    high, low = split(everyone[:, :size])
    index = everyone[:, size, : 2 * slots].astype(jnp.int32)
    pick = jax.nn.one_hot(index, owned, dtype=jnp.bfloat16)
    spread = jnp.swapaxes(pick, 1, 2)

    partial = jnp.dot(waves, rotation, precision=lax.Precision.HIGH, preferred_element_type=jnp.float32)
    turned = lax.psum_scatter(partial, "band", scatter_dimension=1, tiled=True)
    share = width // doms
    columns = lax.all_to_all(turned, "dom", split_axis=1, concat_axis=0, tiled=True)
    columns = columns.reshape(doms, owned, share)
    half = LANES // 2
    columns = jnp.pad(columns, ((0, 0), (0, 0), (0, half - share)))
    columns = jnp.concatenate([columns, columns], axis=2)
    vmem = pl.BlockSpec(memory_space=pltpu.VMEM)
    done = pl.pallas_call(
        functools.partial(filter_kernel, doms, owned, slots, half),
        out_shape=jax.ShapeDtypeStruct((doms, owned, LANES), jnp.float32),
        in_specs=[vmem] * 5,
        out_specs=vmem,
        scratch_shapes=[
            pltpu.VMEM((doms, size, LANES), jnp.bfloat16),
            pltpu.VMEM((doms, 2 * slots, LANES), jnp.bfloat16),
            pltpu.VMEM((doms, owned, LANES), jnp.float32),
            pltpu.VMEM((doms, owned, LANES), jnp.float32),
        ],
        compiler_params=pltpu.CompilerParams(vmem_limit_bytes=56 * 2**20),
        cost_estimate=pl.CostEstimate(
            flops=DEGREE * doms * 4 * size * size * LANES, bytes_accessed=2**24, transcendentals=0
        ),
    )(high, low, pick, spread, columns)
    back = done[:, :, :share].reshape(doms * owned, share)
    return lax.all_to_all(back, "dom", split_axis=0, concat_axis=1, tiled=True)


def solution(mesh):
    in_specs = (
        P("dom", "band"),
        P("dom", None, None),
        P("dom", None),
        P("dom", None, None),
        P("band", None),
    )
    out_specs = P("dom", "band")
    return jax.shard_map(shards, mesh=mesh, in_specs=in_specs, out_specs=out_specs, check_vma=False)
```

```python
import functools

import jax
import jax.numpy as jnp
from jax import lax
from jax.experimental import pallas as pl
from jax.experimental.pallas import tpu as pltpu
from jax.sharding import PartitionSpec as P

DEGREE = 8
LANES = 128
MESH = pl.DeviceIdType.MESH
SPAN = ((0, 96), (96, 64), (160, 48), (208, 32), (240, 16))
ORDER = ((3, 0), (3, 1), (2, 0), (1, 0), (3, 2), (2, 1), (1, 1), (3, 3), (2, 2), (1, 2), (3, 4), (2, 3), (2, 4),
         (1, 3), (1, 4))
FIRST, LINK, HOP, STOP, READY = 4.4, 2.8 / 64, 1.7, 0.2, 21.0
STOPS = (3, 7)
CLOSE = (1, 3, 5, 7)
HALVES = ((0, 136), (136, 64))


centre = 5.5
half_width = 9.5


def split(x):
    high = lax.reduce_precision(x, 8, 7)
    return high.astype(jnp.bfloat16), (x - high).astype(jnp.bfloat16)


def doubled(x, half):
    return x + pltpu.roll(x, half, 1)


def packed(x, half):
    high = x.astype(jnp.bfloat16)
    low = (x - high.astype(jnp.float32)).astype(jnp.bfloat16)
    lane = lax.broadcasted_iota(jnp.int32, x.shape, 1)
    return jnp.where(lane < half, high.astype(jnp.float32), low.astype(jnp.float32)).astype(
        jnp.bfloat16
    )


def mm(a, b):
    return jnp.dot(a, b, preferred_element_type=jnp.float32)


def filter_kernel(doms, owned, slots, half, high, low, pick, spread, start, out, pieces, ghosts, before, image):
    unroll = doms <= 8

    def over(body):
        if unroll:
            for d in range(doms):
                body(d)
        else:
            pl.loop(0, doms)(body)

    def begin(d):
        v = start[d]
        out[d] = v
        before[d] = jnp.zeros_like(v)
        pieces[d, :owned] = packed(v, half)

    over(begin)

    def one(step, _):
        def send(d):
            after = lax.rem(d + 1, doms) if not unroll else (d + 1) % doms
            ahead = lax.rem(d + doms - 1, doms) if not unroll else (d - 1) % doms
            g = mm(pick[d], pieces[d, :owned]).astype(jnp.bfloat16)
            pieces[after, owned : owned + slots] = g[:slots]
            pieces[ahead, owned + slots :] = g[slots:]

        over(send)

        def apply(d):
            x = pieces[d]
            y = mm(high[d], x) + mm(low[d], x)
            y = doubled(y, half)
            image[d] = y[:owned]
            after = lax.rem(d + 1, doms) if not unroll else (d + 1) % doms
            ahead = lax.rem(d + doms - 1, doms) if not unroll else (d - 1) % doms
            r = packed(y[owned:], half)
            ghosts[ahead, :slots] = r[:slots]
            ghosts[after, slots:] = r[slots:]

        over(apply)
        scale = jnp.where(step == 0, 1.0, 2.0)

        def update(d):
            y = image[d] + doubled(mm(spread[d], ghosts[d]), half)
            v = scale * y - before[d]
            before[d] = out[d]
            out[d] = v
            pieces[d, :owned] = packed(v, half)

        over(update)
        return 0

    lax.fori_loop(0, DEGREE, one, 0)


def high_low(x):
    high = x.astype(jnp.bfloat16)
    return high, (x - high.astype(jnp.float32)).astype(jnp.bfloat16)


def fused_kernel(bands, owned, slots, waves_in, cells_in, conn, send, rotation_in, out, *scratch):
    (waves, cells, rotation, load, acc, from_left, from_right, everyone, matrix, pick, spread, pieces, ghosts, image, even, odd,
     gathered, y_high, y_low, p_high, p_low,
     z_send, z_right, z_left, m_send, m_recv, y_send, y_recv) = scratch
    doms = 8
    size = owned + 2 * slots
    rows = owned // 2
    b16 = jnp.bfloat16
    me = lax.axis_index("dom")
    z = lax.axis_index("band")
    core = lax.rem(me, 2)
    place = lax.rem(lax.div(me, 2), 2)
    upper = lax.div(me, 4)
    sib = me + 1 - 2 * core
    x_next = me + 2 - 4 * place
    y_next = me + 4 - 8 * upper
    diag = x_next + 4 - 8 * upper
    across = x_next * (1 - core) + y_next * core
    onward = y_next * (1 - core) + x_next * core

    def seat_of(dom, at):
        return lax.rem(dom - at + doms, doms)

    barrier = pltpu.get_barrier_semaphore()
    for t in range(1, doms):
        pl.semaphore_signal(barrier, inc=1, device_id={"dom": lax.rem(me + t, doms)}, device_id_type=MESH)

    @pl.when(z > 0)
    def _():
        pl.semaphore_signal(barrier, inc=1, device_id={"band": z - 1}, device_id_type=MESH)

    @pl.when(z < bands - 1)
    def _():
        pl.semaphore_signal(barrier, inc=1, device_id={"band": z + 1}, device_id_type=MESH)

    width = waves.shape[1]

    def block(j):
        return pl.ds(j * width, width)

    order = []
    for r in range(bands // 2):
        order += [bands - 1 - r, r]
    loads = [pltpu.make_async_copy(waves_in, waves, load.at[bands + 1])]
    loads += [pltpu.make_async_copy(rotation_in.at[:, block(j)], rotation.at[:, block(j)], load.at[j]) for j in order]
    loads.insert(3, pltpu.make_async_copy(cells_in, cells, load.at[bands]))
    for copy in loads:
        copy.start()

    def rows_of(c):
        return pl.ds(*SPAN[c])

    def to_right(j, c):
        return pltpu.make_async_remote_copy(
            src_ref=acc.at[j, rows_of(c)], dst_ref=from_left.at[j, rows_of(c)], send_sem=z_send.at[j, c],
            recv_sem=z_right.at[j, c], device_id={"band": z + 1}, device_id_type=MESH)

    def to_left(j, c):
        return pltpu.make_async_remote_copy(
            src_ref=acc.at[j, rows_of(c)], dst_ref=from_right.at[j, rows_of(c)], send_sem=z_send.at[j, c],
            recv_sem=z_left.at[j, c], device_id={"band": z - 1}, device_id_type=MESH)

    def send_right(items):
        @pl.when(z == 0)
        def _():
            for j, c in items:
                to_right(j, c).start()

    def send_left(items):
        @pl.when(z == bands - 1)
        def _():
            for j, c in items:
                to_left(bands - 1 - j, c).start()

    loads[0].wait()
    w_high, w_low = high_low(waves[...])

    def partial(j):
        r_high, r_low = high_low(rotation[:, j * width : (j + 1) * width])
        acc[j] = mm(w_high, r_high) + (mm(w_high, r_low) + mm(w_low, r_high))

    loads[1].wait()
    partial(3)
    loads[2].wait()
    partial(0)
    beside = lax.div(z + bands - 1, bands) + lax.div(2 * bands - 2 - z, bands)
    pl.semaphore_wait(barrier, doms - 1 + beside)

    send_right(ORDER[:2])
    send_left(ORDER[:2])

    loads[3].wait()
    node = lax.broadcasted_iota(jnp.int32, (size, conn.shape[1]), 0)
    stacks = [[], [], []]
    gap = jnp.zeros((size, LANES - conn.shape[1]), b16)
    for c in range(cells.shape[1]):
        seat = jnp.where(node == conn[c : c + 1, :], 1.0, 0.0).astype(b16)
        a_high, a_low = high_low(cells[:, c, :])
        b_high, b_low = high_low(mm(seat, a_high) + mm(seat, a_low))
        for stack, part in zip(stacks, (b_high, b_low, seat)):
            stack += [part, gap]
    b_high, b_low, seats = (jnp.concatenate(stack, axis=1) for stack in stacks)
    dims = (((1,), (1,)), ((), ()))
    total = lax.dot_general(b_high, seats, dims, preferred_element_type=jnp.float32) + lax.dot_general(
        b_low, seats, dims, preferred_element_type=jnp.float32)
    r_at = lax.broadcasted_iota(jnp.int32, (size, size), 0)
    c_at = lax.broadcasted_iota(jnp.int32, (size, size), 1)
    shift = jnp.where((r_at == c_at) & (r_at < owned), centre, 0.0)
    total = (total - shift) / half_width
    i_at = lax.broadcasted_iota(jnp.int32, (rows, rows), 0)
    j_at = lax.broadcasted_iota(jnp.int32, (rows, rows), 1)
    quarter = rows // 2
    one, two, three = slice(0, rows), slice(rows, 2 * rows), slice(2 * rows, 3 * rows)
    base, tail = slice(rows, rows + quarter), rows + quarter
    corner = total[three, three]
    top, bottom = corner[:quarter], pltpu.roll(corner[quarter:], quarter, 1)
    mixed = jnp.where(i_at <= j_at, total[one, one], total[two, two])
    everyone[0, one, one] = total[one, two]
    everyone[0, one, two] = total[one, three]
    everyone[0, one, three] = total[two, three]
    everyone[0, base, one] = mixed[:quarter]
    everyone[0, base, two] = mixed[quarter:]
    everyone[0, base, three] = jnp.where((i_at <= j_at)[:quarter], top, bottom)
    everyone[0, tail:] = jnp.zeros((8, size), jnp.float32)
    everyone[0, tail : tail + 2, :slots] = send[0].astype(jnp.float32)
    everyone[0, tail : tail + 1, two] = jnp.sum(
        jnp.where(i_at == j_at, total[two, two], 0.0), axis=0, keepdims=True)
    everyone[0, tail : tail + 1, three] = jnp.sum(jnp.where(i_at == j_at, corner, 0.0), axis=0, keepdims=True)

    def m_copy(h, dom, to, k):
        return pltpu.make_async_remote_copy(
            src_ref=everyone.at[seat_of(dom, me), pl.ds(*HALVES[h])],
            dst_ref=everyone.at[seat_of(dom, to), pl.ds(*HALVES[h])], send_sem=m_send.at[h, k],
            recv_sem=m_recv.at[h, seat_of(dom, to)], device_id={"dom": to}, device_id_type=MESH)

    def m_wait(h, dom):
        part = everyone.at[seat_of(dom, me), pl.ds(*HALVES[h])]
        pltpu.make_async_remote_copy(
            src_ref=part, dst_ref=part, send_sem=m_send.at[h, 0], recv_sem=m_recv.at[h, seat_of(dom, me)],
            device_id={"dom": sib}, device_id_type=MESH).wait_recv()

    def y_copy(c, dom, to, k):
        return pltpu.make_async_remote_copy(
            src_ref=gathered.at[seat_of(dom, me), rows_of(c)], dst_ref=gathered.at[seat_of(dom, to), rows_of(c)],
            send_sem=y_send.at[c, k], recv_sem=y_recv.at[c, seat_of(dom, to)], device_id={"dom": to},
            device_id_type=MESH)

    def y_wait(c, dom):
        part = gathered.at[seat_of(dom, me), rows_of(c)]
        pltpu.make_async_remote_copy(
            src_ref=part, dst_ref=part, send_sem=y_send.at[c, 0], recv_sem=y_recv.at[c, seat_of(dom, me)],
            device_id={"dom": sib}, device_id_type=MESH).wait_recv()

    unsent = []

    def go(copy):
        copy.start()
        unsent.append(copy)

    def first_hop(copy):
        go(copy(me, x_next, 0))
        go(copy(me, y_next, 1))
        go(copy(me, sib, 2))

    def second_hop(copy, wait):
        wait(x_next)
        wait(y_next)
        go(copy(across, onward, 3))
        go(copy(x_next, sib, 4))
        go(copy(y_next, sib, 5))

    def third_hop(copy, wait):
        wait(diag)
        go(copy(diag, sib, 6))

    away = [sib, x_next + 1 - 2 * core, y_next + 1 - 2 * core, diag + 1 - 2 * core]

    copies = [functools.partial(m_copy, h) for h in range(2)]
    waits = [functools.partial(m_wait, h) for h in range(2)]
    for h in range(2):
        first_hop(copies[h])

    for copy in loads[4:]:
        copy.wait()
    partial(2)
    partial(1)
    send_right(ORDER[2:])
    send_left(ORDER[2:])

    def relay(k, hop):
        def right(j, c):
            to_right(j, c).wait_recv()
            acc[j, rows_of(c)] = acc[j, rows_of(c)] + from_left[j, rows_of(c)]
            to_right(j, c).start()

        def left(j, c):
            to_left(j, c).wait_recv()
            acc[j, rows_of(c)] = acc[j, rows_of(c)] + from_right[j, rows_of(c)]
            to_left(j, c).start()

        last = bands - 1
        j, c = ORDER[k]

        @pl.when(z == hop)
        def _():
            right(j, c)

        @pl.when(z == last - hop)
        def _():
            left(last - j, c)

    def finish(c):
        part = rows_of(c)
        gathered[0, part] = acc[z, part]

        @pl.when(z > 0)
        def _():
            to_right(z, c).wait_recv()
            gathered[0, part] = gathered[0, part] + from_left[z, part]

        @pl.when(z < bands - 1)
        def _():
            to_left(z, c).wait_recv()
            gathered[0, part] = gathered[0, part] + from_right[z, part]

        if c == len(SPAN) - 1:
            for k, dom in enumerate((diag, away[3], x_next, y_next, away[1], away[2], sib)):
                go(y_copy(c, me, dom, k))
        else:
            for k, dom in enumerate((diag, x_next, y_next, sib)):
                go(y_copy(c, me, dom, k))

    def pass_on(c):
        for k, dom in enumerate((x_next, y_next, diag)):
            y_wait(c, dom)
            go(y_copy(c, dom, sib, 4 + k))

    def y_split(c):
        others = (x_next, y_next, diag) if c == len(SPAN) - 1 else ()
        for dom in (*away, *others):
            y_wait(c, dom)
        first, count = SPAN[c]
        for d in range(doms):
            high, low = high_low(gathered[d, first : first + count])
            at = doms * first + d * count
            y_high[at : at + count] = high
            y_low[at : at + count] = low

    def prepare(d):
        straight = jnp.concatenate([everyone[d, base, one], everyone[d, base, two]], axis=0)
        across_it = jnp.transpose(straight)
        piece = everyone[d, base, three]
        folded = jnp.concatenate([piece, pltpu.roll(piece, quarter, 1)], axis=0)
        unfolded = jnp.transpose(folded)
        second_line, third_line = everyone[d, tail : tail + 1, two], everyone[d, tail : tail + 1, three]
        first_block = jnp.where(i_at <= j_at, straight, across_it)
        second_block = jnp.where(i_at > j_at, straight, jnp.where(i_at < j_at, across_it, second_line))
        direct = ((i_at < quarter) & (i_at <= j_at)) | ((j_at >= quarter) & (i_at > j_at))
        third_block = jnp.where(
            direct, folded, jnp.where((i_at == j_at) & (i_at >= quarter), third_line, unfolded))
        ab, ac, bc = everyone[d, one, one], everyone[d, one, two], everyone[d, one, three]
        lines = (
            (one, (first_block, ab, ac)),
            (two, (jnp.transpose(ab), second_block, bc)),
            (three, (jnp.transpose(ac), jnp.transpose(bc), third_block)),
        )
        for line, blocks in lines:
            m_high, m_low = high_low(jnp.concatenate(blocks, axis=1))
            matrix[d, line, :size] = m_high
            matrix[d, line, size : 2 * size] = m_low
            matrix[d, line, 2 * size :] = m_high
        tile = everyone[d, tail:, :LANES]
        other = pltpu.roll(tile, slots, 1)
        first_lanes = lax.broadcasted_iota(jnp.int32, (1, LANES), 1) < slots
        row = jnp.where(first_lanes, tile[0:1], other[1:2]).astype(jnp.int32)
        at = lax.broadcasted_iota(jnp.int32, (owned, LANES), 0)
        hot = jnp.where(at == row, 1.0, 0.0)
        spread[d, :, :LANES] = hot.astype(b16)
        spread[d, :, LANES:] = hot.astype(b16)
        pick[d] = jnp.transpose(hot).astype(b16)

    agenda, late = [], []
    arrival, clock = {}, FIRST
    for k, (j, c) in enumerate(ORDER):
        clock += LINK * SPAN[c][1]
        arrival[j, c, 1] = clock
        for hop in range(1, j):
            agenda.append((arrival[j, c, hop] + STOP, relay, (k, hop)))
            arrival[j, c, hop + 1] = arrival[j, c, hop] + STOP + LINK * SPAN[c][1] + HOP
    for c, (first, count) in enumerate(SPAN):
        done = max(arrival[1, c, 1], arrival[2, c, 2], arrival[3, c, 3]) + (2 * STOP if c else 2.0)
        agenda.append((done, finish, (c,)))
        done += 2 * LINK * count + HOP + 1.0
        if c < len(SPAN) - 1:
            agenda.append((done, pass_on, (c,)))
        agenda.append((done + 2.0, y_split, (c,)))
        if c >= len(SPAN) - 3:
            late.append(agenda.pop())
            if c == len(SPAN) - 2:
                late.insert(0, agenda.pop())
    agenda.sort(key=lambda item: item[0])

    def tick(now):
        while agenda and agenda[0][0] <= now:
            _, act, details = agenda.pop(0)
            act(*details)

    pieces[...] = jnp.zeros_like(pieces)
    ghosts[...] = jnp.zeros_like(ghosts)
    eye = jnp.where(
        lax.broadcasted_iota(jnp.int32, (owned, owned), 0) == lax.broadcasted_iota(jnp.int32, (owned, owned), 1),
        1.0, 0.0)
    even[:owned] = eye
    pieces[0, :owned] = eye.astype(b16)
    pieces[0, size : size + owned] = eye.astype(b16)
    prepare(0)

    def ready(dom):
        prepare(seat_of(dom, me))

    for wait in waits:
        wait(sib)
    ready(sib)
    tick(READY - 11.0)
    second_hop(copies[0], waits[0])
    tick(READY - 9.0)
    second_hop(copies[1], waits[1])
    ready(x_next)
    ready(y_next)
    tick(READY - 6.0)
    third_hop(copies[0], waits[0])
    for dom in away[1:3]:
        for wait in waits:
            wait(dom)
        ready(dom)
    tick(READY - 4.0)
    third_hop(copies[1], waits[1])
    ready(diag)
    tick(READY - 2.0)
    for wait in waits:
        wait(away[3])
    ready(away[3])

    every = list(range(doms))
    held = [[0], [6, 7, 0, 1, 2]]
    busy = [[7, 0, 1], [5, 6, 7, 0, 1, 2, 3]]

    now = [READY]

    def spend(time):
        now[0] += time

    def advance(k):
        end = k == DEGREE
        source = held[k - 1] if k <= 2 else every
        active = busy[k - 1] if k <= 2 else every
        result = held[k] if k < 2 else every
        old = [] if k == 1 else held[k - 2] if k <= 3 else every
        store = odd if k % 2 else even
        for d in source:
            after, ahead = (d + 1) % doms, (d - 1) % doms
            for at, bases in ((0, (0, size)), (2 * size, (2 * size,))):
                g = mm(pick[d], pieces[d, at : at + owned]).astype(b16)
                for base in bases:
                    pieces[after, base + owned : base + owned + slots] = g[:slots]
                    pieces[ahead, base + owned + slots : base + size] = g[slots:]
        spend(0.05 * len(source))
        for d in active:
            after, ahead = (d + 1) % doms, (d - 1) % doms
            if k > 1:
                y = mm(matrix[d], pieces[d])
            elif d == 0:
                y = matrix[d, :, :owned].astype(jnp.float32) + matrix[d, :, size : size + owned].astype(jnp.float32)
            else:
                beyond = pieces[d, owned:size]
                y = mm(matrix[d, :, owned:size], beyond) + mm(matrix[d, :, size + owned : 2 * size], beyond)
            image[d] = y[:owned]
            high, low = high_low(y[owned:])
            ghosts[ahead, :slots] = high[:slots]
            ghosts[ahead, 2 * slots : 3 * slots] = low[:slots]
            ghosts[after, slots : 2 * slots] = high[slots:]
            ghosts[after, 3 * slots :] = low[slots:]
            spend(0.28 if k > 1 else 0.1)
            if d in (CLOSE if k >= DEGREE - 1 else STOPS):
                tick(now[0])
        for d in result:
            home = slice(d * owned, (d + 1) * owned)
            y = mm(spread[d], ghosts[d])
            if d in active:
                y = y + image[d]
            v = y if k == 1 else 2.0 * y
            if d in old:
                v = v - store[home]
            if end:
                for first, count in SPAN:
                    at = doms * first + d * count
                    odd[at : at + count] = v[first : first + count]
            else:
                store[home] = v
                high, low = high_low(v)
                pieces[d, :owned] = high
                pieces[d, size : size + owned] = high
                pieces[d, 2 * size : 2 * size + owned] = low
        spend(0.055 * len(result))

    for k in range(1, DEGREE + 1):
        advance(k)
    tick(1000.0)
    for d in range(doms):
        high, low = high_low(jnp.transpose(odd[d * owned : (d + 1) * owned]))
        p_high[:, d * owned : (d + 1) * owned] = high
        p_low[:, d * owned : (d + 1) * owned] = low

    def product(at):
        high, low = y_high[at], y_low[at]
        return mm(p_high[:, at], high) + (mm(p_high[:, at], low) + mm(p_low[:, at], high))

    bulk = doms * SPAN[-2][0]
    for _, act, details in late[:2]:
        act(*details)
    out[...] = product(slice(0, bulk))
    for _, act, details in late[2:]:
        act(*details)
    out[...] = out[...] + product(slice(bulk, doms * owned))

    for copy in unsent:
        copy.wait_send()
    for j in range(bands):
        for c in range(len(SPAN)):
            @pl.when(z < j)
            def _():
                to_right(j, c).wait_send()

            @pl.when(z > j)
            def _():
                to_left(j, c).wait_send()


def fused(waves, cell_matrix, connect, send_index, rotation):
    owned, width = waves.shape
    slots = send_index.shape[2]
    bands = lax.axis_size("band")
    size = owned + 2 * slots
    doms = 8
    vmem = pl.BlockSpec(memory_space=pltpu.VMEM)
    anywhere = pl.BlockSpec(memory_space=pl.ANY)
    cells = jnp.swapaxes(cell_matrix, 0, 1)
    f32, b16 = jnp.float32, jnp.bfloat16
    dma = pltpu.SemaphoreType.DMA
    return pl.pallas_call(
        functools.partial(fused_kernel, bands, owned, slots),
        out_shape=jax.ShapeDtypeStruct((owned, width), f32),
        in_specs=[anywhere, anywhere, vmem, vmem, anywhere],
        out_specs=vmem,
        scratch_shapes=[
            pltpu.VMEM((owned, width), f32),
            pltpu.VMEM(cells.shape, f32),
            pltpu.VMEM(rotation.shape, f32),
            dma((bands + 2,)),
            pltpu.VMEM((bands, owned, width), f32),
            pltpu.VMEM((bands, owned, width), f32),
            pltpu.VMEM((bands, owned, width), f32),
            pltpu.VMEM((doms, HALVES[1][0] + HALVES[1][1], size), f32),
            pltpu.VMEM((doms, size, 3 * size), b16),
            pltpu.VMEM((doms, 2 * slots, owned), b16),
            pltpu.VMEM((doms, owned, 4 * slots), b16),
            pltpu.VMEM((doms, 3 * size, owned), b16),
            pltpu.VMEM((doms, 4 * slots, owned), b16),
            pltpu.VMEM((doms, owned, owned), f32),
            pltpu.VMEM((doms * owned, owned), f32),
            pltpu.VMEM((doms * owned, owned), f32),
            pltpu.VMEM((doms, owned, width), f32),
            pltpu.VMEM((doms * owned, width), b16),
            pltpu.VMEM((doms * owned, width), b16),
            pltpu.VMEM((owned, doms * owned), b16),
            pltpu.VMEM((owned, doms * owned), b16),
            dma((bands, len(SPAN))), dma((bands, len(SPAN))), dma((bands, len(SPAN))),
            dma((2, 7)), dma((2, doms)),
            dma((len(SPAN), 7)), dma((len(SPAN), doms)),
        ],
        compiler_params=pltpu.CompilerParams(
            vmem_limit_bytes=60 * 2**20, collective_id=0, has_side_effects=True),
        cost_estimate=pl.CostEstimate(
            flops=DEGREE * doms * 6 * size * size * owned, bytes_accessed=2**24, transcendentals=0),
    )(waves, cells, connect, send_index, rotation)


def shards(waves, cell_matrix, connect, send_index, rotation):
    owned = waves.shape[0]
    width = waves.shape[1]
    slots = send_index.shape[2]
    doms = lax.axis_size("dom")
    if doms == 8 and width == doms * LANES // 2 and 2 * slots == LANES and owned == 2 * LANES and lax.axis_size("band") == 4:
        return fused(waves, cell_matrix, connect, send_index, rotation)
    size = owned + 2 * slots
    seat = jax.nn.one_hot(connect, size, dtype=jnp.float32)
    half_way = jnp.einsum("cij,cjn->cin", cell_matrix, seat, precision=lax.Precision.HIGH)
    local = jnp.einsum("cim,cin->mn", seat, half_way, precision=lax.Precision.HIGH)
    node = jnp.arange(size)
    shift = jnp.where((node[:, None] == node[None, :]) & (node[:, None] < owned), centre, 0.0)
    local = (local - shift) / half_width
    row = jnp.zeros((8, size), jnp.float32).at[0, : 2 * slots].set(
        send_index.reshape(-1).astype(jnp.float32)
    )
    everyone = lax.all_gather(jnp.concatenate([local, row], axis=0), "dom")
    high, low = split(everyone[:, :size])
    index = everyone[:, size, : 2 * slots].astype(jnp.int32)
    pick = jax.nn.one_hot(index, owned, dtype=jnp.bfloat16)
    spread = jnp.swapaxes(pick, 1, 2)

    partial = jnp.dot(waves, rotation, precision=lax.Precision.HIGH, preferred_element_type=jnp.float32)
    turned = lax.psum_scatter(partial, "band", scatter_dimension=1, tiled=True)
    share = width // doms
    columns = lax.all_to_all(turned, "dom", split_axis=1, concat_axis=0, tiled=True)
    columns = columns.reshape(doms, owned, share)
    half = LANES // 2
    columns = jnp.pad(columns, ((0, 0), (0, 0), (0, half - share)))
    columns = jnp.concatenate([columns, columns], axis=2)
    vmem = pl.BlockSpec(memory_space=pltpu.VMEM)
    done = pl.pallas_call(
        functools.partial(filter_kernel, doms, owned, slots, half),
        out_shape=jax.ShapeDtypeStruct((doms, owned, LANES), jnp.float32),
        in_specs=[vmem] * 5,
        out_specs=vmem,
        scratch_shapes=[
            pltpu.VMEM((doms, size, LANES), jnp.bfloat16),
            pltpu.VMEM((doms, 2 * slots, LANES), jnp.bfloat16),
            pltpu.VMEM((doms, owned, LANES), jnp.float32),
            pltpu.VMEM((doms, owned, LANES), jnp.float32),
        ],
        compiler_params=pltpu.CompilerParams(vmem_limit_bytes=56 * 2**20),
        cost_estimate=pl.CostEstimate(
            flops=DEGREE * doms * 4 * size * size * LANES, bytes_accessed=2**24, transcendentals=0
        ),
    )(high, low, pick, spread, columns)
    back = done[:, :, :share].reshape(doms * owned, share)
    return lax.all_to_all(back, "dom", split_axis=0, concat_axis=1, tiled=True)


def solution(mesh):
    in_specs = (
        P("dom", "band"),
        P("dom", None, None),
        P("dom", None),
        P("dom", None, None),
        P("band", None),
    )
    out_specs = P("dom", "band")
    return jax.shard_map(shards, mesh=mesh, in_specs=in_specs, out_specs=out_specs, check_vma=False)
```

```python
import functools

import jax
import jax.numpy as jnp
from jax import lax
from jax.experimental import pallas as pl
from jax.experimental.pallas import tpu as pltpu
from jax.sharding import PartitionSpec as P

DEGREE = 8
LANES = 128
MESH = pl.DeviceIdType.MESH
SPAN = ((0, 96), (96, 64), (160, 48), (208, 32), (240, 16))
ORDER = ((3, 0), (3, 1), (2, 0), (1, 0), (3, 2), (2, 1), (1, 1), (3, 3), (2, 2), (1, 2), (3, 4), (2, 3), (2, 4),
         (1, 3), (1, 4))
FIRST, LINK, HOP, STOP, READY = 4.4, 2.8 / 64, 1.7, 0.2, 21.0
STOPS = (3, 7)
CLOSE = (0, 2, 4, 6, 7)
HALVES = ((0, 152), (152, 48))


centre = 5.5
half_width = 9.5


def split(x):
    high = lax.reduce_precision(x, 8, 7)
    return high.astype(jnp.bfloat16), (x - high).astype(jnp.bfloat16)


def doubled(x, half):
    return x + pltpu.roll(x, half, 1)


def packed(x, half):
    high = x.astype(jnp.bfloat16)
    low = (x - high.astype(jnp.float32)).astype(jnp.bfloat16)
    lane = lax.broadcasted_iota(jnp.int32, x.shape, 1)
    return jnp.where(lane < half, high.astype(jnp.float32), low.astype(jnp.float32)).astype(
        jnp.bfloat16
    )


def mm(a, b):
    return jnp.dot(a, b, preferred_element_type=jnp.float32)


def filter_kernel(doms, owned, slots, half, high, low, pick, spread, start, out, pieces, ghosts, before, image):
    unroll = doms <= 8

    def over(body):
        if unroll:
            for d in range(doms):
                body(d)
        else:
            pl.loop(0, doms)(body)

    def begin(d):
        v = start[d]
        out[d] = v
        before[d] = jnp.zeros_like(v)
        pieces[d, :owned] = packed(v, half)

    over(begin)

    def one(step, _):
        def send(d):
            after = lax.rem(d + 1, doms) if not unroll else (d + 1) % doms
            ahead = lax.rem(d + doms - 1, doms) if not unroll else (d - 1) % doms
            g = mm(pick[d], pieces[d, :owned]).astype(jnp.bfloat16)
            pieces[after, owned : owned + slots] = g[:slots]
            pieces[ahead, owned + slots :] = g[slots:]

        over(send)

        def apply(d):
            x = pieces[d]
            y = mm(high[d], x) + mm(low[d], x)
            y = doubled(y, half)
            image[d] = y[:owned]
            after = lax.rem(d + 1, doms) if not unroll else (d + 1) % doms
            ahead = lax.rem(d + doms - 1, doms) if not unroll else (d - 1) % doms
            r = packed(y[owned:], half)
            ghosts[ahead, :slots] = r[:slots]
            ghosts[after, slots:] = r[slots:]

        over(apply)
        scale = jnp.where(step == 0, 1.0, 2.0)

        def update(d):
            y = image[d] + doubled(mm(spread[d], ghosts[d]), half)
            v = scale * y - before[d]
            before[d] = out[d]
            out[d] = v
            pieces[d, :owned] = packed(v, half)

        over(update)
        return 0

    lax.fori_loop(0, DEGREE, one, 0)


def high_low(x):
    high = x.astype(jnp.bfloat16)
    return high, (x - high.astype(jnp.float32)).astype(jnp.bfloat16)


def fused_kernel(bands, owned, slots, waves_in, cells_in, conn, send, rotation_in, out, *scratch):
    (waves, cells, rotation, load, acc, from_left, from_right, everyone, matrix, pick, spread, pieces, ghosts, image, even, odd,
     gathered, y_high, y_low, p_high, p_low,
     z_send, z_right, z_left, m_send, m_recv, y_send, y_recv) = scratch
    doms = 8
    size = owned + 2 * slots
    rows = owned // 2
    b16 = jnp.bfloat16
    me = lax.axis_index("dom")
    z = lax.axis_index("band")
    core = lax.rem(me, 2)
    place = lax.rem(lax.div(me, 2), 2)
    upper = lax.div(me, 4)
    sib = me + 1 - 2 * core
    x_next = me + 2 - 4 * place
    y_next = me + 4 - 8 * upper
    diag = x_next + 4 - 8 * upper
    across = x_next * (1 - core) + y_next * core
    onward = y_next * (1 - core) + x_next * core

    def seat_of(dom, at):
        return lax.rem(dom - at + doms, doms)

    barrier = pltpu.get_barrier_semaphore()
    for t in range(1, doms):
        pl.semaphore_signal(barrier, inc=1, device_id={"dom": lax.rem(me + t, doms)}, device_id_type=MESH)

    @pl.when(z > 0)
    def _():
        pl.semaphore_signal(barrier, inc=1, device_id={"band": z - 1}, device_id_type=MESH)

    @pl.when(z < bands - 1)
    def _():
        pl.semaphore_signal(barrier, inc=1, device_id={"band": z + 1}, device_id_type=MESH)

    width = waves.shape[1]

    def block(j):
        return pl.ds(j * width, width)

    order = []
    for r in range(bands // 2):
        order += [bands - 1 - r, r]
    loads = [pltpu.make_async_copy(waves_in, waves, load.at[bands + 1])]
    loads += [pltpu.make_async_copy(rotation_in.at[:, block(j)], rotation.at[:, block(j)], load.at[j]) for j in order]
    loads.insert(3, pltpu.make_async_copy(cells_in, cells, load.at[bands]))
    for copy in loads:
        copy.start()

    def rows_of(c):
        return pl.ds(*SPAN[c])

    def to_right(j, c):
        return pltpu.make_async_remote_copy(
            src_ref=acc.at[j, rows_of(c)], dst_ref=from_left.at[j, rows_of(c)], send_sem=z_send.at[j, c],
            recv_sem=z_right.at[j, c], device_id={"band": z + 1}, device_id_type=MESH)

    def to_left(j, c):
        return pltpu.make_async_remote_copy(
            src_ref=acc.at[j, rows_of(c)], dst_ref=from_right.at[j, rows_of(c)], send_sem=z_send.at[j, c],
            recv_sem=z_left.at[j, c], device_id={"band": z - 1}, device_id_type=MESH)

    def send_right(items):
        @pl.when(z == 0)
        def _():
            for j, c in items:
                to_right(j, c).start()

    def send_left(items):
        @pl.when(z == bands - 1)
        def _():
            for j, c in items:
                to_left(bands - 1 - j, c).start()

    loads[0].wait()
    w_high, w_low = high_low(waves[...])

    def partial(j):
        r_high, r_low = high_low(rotation[:, j * width : (j + 1) * width])
        acc[j] = mm(w_high, r_high) + (mm(w_high, r_low) + mm(w_low, r_high))

    loads[1].wait()
    partial(3)
    loads[2].wait()
    partial(0)
    beside = lax.div(z + bands - 1, bands) + lax.div(2 * bands - 2 - z, bands)
    pl.semaphore_wait(barrier, doms - 1 + beside)

    send_right(ORDER[:2])
    send_left(ORDER[:2])

    loads[3].wait()
    node = lax.broadcasted_iota(jnp.int32, (size, conn.shape[1]), 0)
    stacks = [[], [], []]
    gap = jnp.zeros((size, LANES - conn.shape[1]), b16)
    for c in range(cells.shape[1]):
        seat = jnp.where(node == conn[c : c + 1, :], 1.0, 0.0).astype(b16)
        a_high, a_low = high_low(cells[:, c, :])
        b_high, b_low = high_low(mm(seat, a_high) + mm(seat, a_low))
        for stack, part in zip(stacks, (b_high, b_low, seat)):
            stack += [part, gap]
    b_high, b_low, seats = (jnp.concatenate(stack, axis=1) for stack in stacks)
    dims = (((1,), (1,)), ((), ()))
    total = lax.dot_general(b_high, seats, dims, preferred_element_type=jnp.float32) + lax.dot_general(
        b_low, seats, dims, preferred_element_type=jnp.float32)
    r_at = lax.broadcasted_iota(jnp.int32, (size, size), 0)
    c_at = lax.broadcasted_iota(jnp.int32, (size, size), 1)
    shift = jnp.where((r_at == c_at) & (r_at < owned), centre, 0.0)
    total = (total - shift) / half_width
    i_at = lax.broadcasted_iota(jnp.int32, (rows, rows), 0)
    j_at = lax.broadcasted_iota(jnp.int32, (rows, rows), 1)
    quarter = rows // 2
    one, two, three = slice(0, rows), slice(rows, 2 * rows), slice(2 * rows, 3 * rows)
    base, tail = slice(rows, rows + quarter), rows + quarter
    corner = total[three, three]
    top, bottom = corner[:quarter], pltpu.roll(corner[quarter:], quarter, 1)
    mixed = jnp.where(i_at <= j_at, total[one, one], total[two, two])
    everyone[0, one, one] = total[one, two]
    everyone[0, one, two] = total[one, three]
    everyone[0, one, three] = total[two, three]
    everyone[0, base, one] = mixed[:quarter]
    everyone[0, base, two] = mixed[quarter:]
    everyone[0, base, three] = jnp.where((i_at <= j_at)[:quarter], top, bottom)
    everyone[0, tail:] = jnp.zeros((8, size), jnp.float32)
    everyone[0, tail : tail + 2, :slots] = send[0].astype(jnp.float32)
    everyone[0, tail : tail + 1, two] = jnp.sum(
        jnp.where(i_at == j_at, total[two, two], 0.0), axis=0, keepdims=True)
    everyone[0, tail : tail + 1, three] = jnp.sum(jnp.where(i_at == j_at, corner, 0.0), axis=0, keepdims=True)

    def m_copy(h, dom, to, k):
        return pltpu.make_async_remote_copy(
            src_ref=everyone.at[seat_of(dom, me), pl.ds(*HALVES[h])],
            dst_ref=everyone.at[seat_of(dom, to), pl.ds(*HALVES[h])], send_sem=m_send.at[h, k],
            recv_sem=m_recv.at[h, seat_of(dom, to)], device_id={"dom": to}, device_id_type=MESH)

    def m_wait(h, dom):
        part = everyone.at[seat_of(dom, me), pl.ds(*HALVES[h])]
        pltpu.make_async_remote_copy(
            src_ref=part, dst_ref=part, send_sem=m_send.at[h, 0], recv_sem=m_recv.at[h, seat_of(dom, me)],
            device_id={"dom": sib}, device_id_type=MESH).wait_recv()

    def y_copy(c, dom, to, k):
        return pltpu.make_async_remote_copy(
            src_ref=gathered.at[seat_of(dom, me), rows_of(c)], dst_ref=gathered.at[seat_of(dom, to), rows_of(c)],
            send_sem=y_send.at[c, k], recv_sem=y_recv.at[c, seat_of(dom, to)], device_id={"dom": to},
            device_id_type=MESH)

    def y_wait(c, dom):
        part = gathered.at[seat_of(dom, me), rows_of(c)]
        pltpu.make_async_remote_copy(
            src_ref=part, dst_ref=part, send_sem=y_send.at[c, 0], recv_sem=y_recv.at[c, seat_of(dom, me)],
            device_id={"dom": sib}, device_id_type=MESH).wait_recv()

    unsent = []

    def go(copy):
        copy.start()
        unsent.append(copy)

    def first_hop(copy):
        go(copy(me, x_next, 0))
        go(copy(me, y_next, 1))
        go(copy(me, sib, 2))

    def second_hop(copy, wait):
        wait(x_next)
        wait(y_next)
        go(copy(across, onward, 3))
        go(copy(x_next, sib, 4))
        go(copy(y_next, sib, 5))

    def third_hop(copy, wait):
        wait(diag)
        go(copy(diag, sib, 6))

    away = [sib, x_next + 1 - 2 * core, y_next + 1 - 2 * core, diag + 1 - 2 * core]

    copies = [functools.partial(m_copy, h) for h in range(2)]
    waits = [functools.partial(m_wait, h) for h in range(2)]
    for h in range(2):
        first_hop(copies[h])

    for copy in loads[4:]:
        copy.wait()
    partial(2)
    partial(1)
    send_right(ORDER[2:])
    send_left(ORDER[2:])

    def relay(k, hop):
        def right(j, c):
            to_right(j, c).wait_recv()
            acc[j, rows_of(c)] = acc[j, rows_of(c)] + from_left[j, rows_of(c)]
            to_right(j, c).start()

        def left(j, c):
            to_left(j, c).wait_recv()
            acc[j, rows_of(c)] = acc[j, rows_of(c)] + from_right[j, rows_of(c)]
            to_left(j, c).start()

        last = bands - 1
        j, c = ORDER[k]

        @pl.when(z == hop)
        def _():
            right(j, c)

        @pl.when(z == last - hop)
        def _():
            left(last - j, c)

    def finish(c):
        part = rows_of(c)
        gathered[0, part] = acc[z, part]

        @pl.when(z > 0)
        def _():
            to_right(z, c).wait_recv()
            gathered[0, part] = gathered[0, part] + from_left[z, part]

        @pl.when(z < bands - 1)
        def _():
            to_left(z, c).wait_recv()
            gathered[0, part] = gathered[0, part] + from_right[z, part]

        if c == len(SPAN) - 1:
            for k, dom in enumerate((diag, away[3], x_next, y_next, away[1], away[2], sib)):
                go(y_copy(c, me, dom, k))
        else:
            for k, dom in enumerate((diag, x_next, y_next, sib)):
                go(y_copy(c, me, dom, k))

    def pass_on(c):
        for k, dom in enumerate((x_next, y_next, diag)):
            y_wait(c, dom)
            go(y_copy(c, dom, sib, 4 + k))

    def y_split(c):
        others = (x_next, y_next, diag) if c == len(SPAN) - 1 else ()
        for dom in (*away, *others):
            y_wait(c, dom)
        first, count = SPAN[c]
        for d in range(doms):
            high, low = high_low(gathered[d, first : first + count])
            at = doms * first + d * count
            y_high[at : at + count] = high
            y_low[at : at + count] = low

    def prepare(d):
        straight = jnp.concatenate([everyone[d, base, one], everyone[d, base, two]], axis=0)
        across_it = jnp.transpose(straight)
        piece = everyone[d, base, three]
        folded = jnp.concatenate([piece, pltpu.roll(piece, quarter, 1)], axis=0)
        unfolded = jnp.transpose(folded)
        second_line, third_line = everyone[d, tail : tail + 1, two], everyone[d, tail : tail + 1, three]
        first_block = jnp.where(i_at <= j_at, straight, across_it)
        second_block = jnp.where(i_at > j_at, straight, jnp.where(i_at < j_at, across_it, second_line))
        direct = ((i_at < quarter) & (i_at <= j_at)) | ((j_at >= quarter) & (i_at > j_at))
        third_block = jnp.where(
            direct, folded, jnp.where((i_at == j_at) & (i_at >= quarter), third_line, unfolded))
        ab, ac, bc = everyone[d, one, one], everyone[d, one, two], everyone[d, one, three]
        lines = (
            (one, (first_block, ab, ac)),
            (two, (jnp.transpose(ab), second_block, bc)),
            (three, (jnp.transpose(ac), jnp.transpose(bc), third_block)),
        )
        for line, blocks in lines:
            m_high, m_low = high_low(jnp.concatenate(blocks, axis=1))
            matrix[d, line, :size] = m_high
            matrix[d, line, size : 2 * size] = m_low
            matrix[d, line, 2 * size :] = m_high
        tile = everyone[d, tail:, :LANES]
        other = pltpu.roll(tile, slots, 1)
        first_lanes = lax.broadcasted_iota(jnp.int32, (1, LANES), 1) < slots
        row = jnp.where(first_lanes, tile[0:1], other[1:2]).astype(jnp.int32)
        at = lax.broadcasted_iota(jnp.int32, (owned, LANES), 0)
        hot = jnp.where(at == row, 1.0, 0.0)
        spread[d, :, :LANES] = hot.astype(b16)
        spread[d, :, LANES:] = hot.astype(b16)
        pick[d] = jnp.transpose(hot).astype(b16)

    agenda, late = [], []
    arrival, clock = {}, FIRST
    for k, (j, c) in enumerate(ORDER):
        clock += LINK * SPAN[c][1]
        arrival[j, c, 1] = clock
        for hop in range(1, j):
            agenda.append((arrival[j, c, hop] + STOP, relay, (k, hop)))
            arrival[j, c, hop + 1] = arrival[j, c, hop] + STOP + LINK * SPAN[c][1] + HOP
    for c, (first, count) in enumerate(SPAN):
        done = max(arrival[1, c, 1], arrival[2, c, 2], arrival[3, c, 3]) + (2 * STOP if c else 2.0)
        agenda.append((done, finish, (c,)))
        done += 2 * LINK * count + HOP + 1.0
        if c < len(SPAN) - 1:
            agenda.append((done, pass_on, (c,)))
        agenda.append((done + 2.0, y_split, (c,)))
        if c >= len(SPAN) - 3:
            late.append(agenda.pop())
            if c == len(SPAN) - 2:
                late.insert(0, agenda.pop())
    agenda.sort(key=lambda item: item[0])

    def tick(now):
        while agenda and agenda[0][0] <= now:
            _, act, details = agenda.pop(0)
            act(*details)

    pieces[...] = jnp.zeros_like(pieces)
    ghosts[...] = jnp.zeros_like(ghosts)
    eye = jnp.where(
        lax.broadcasted_iota(jnp.int32, (owned, owned), 0) == lax.broadcasted_iota(jnp.int32, (owned, owned), 1),
        1.0, 0.0)
    even[:owned] = eye
    pieces[0, :owned] = eye.astype(b16)
    pieces[0, size : size + owned] = eye.astype(b16)
    prepare(0)

    def ready(dom):
        prepare(seat_of(dom, me))

    for wait in waits:
        wait(sib)
    ready(sib)
    tick(READY - 11.0)
    second_hop(copies[0], waits[0])
    tick(READY - 9.0)
    second_hop(copies[1], waits[1])
    ready(x_next)
    ready(y_next)
    tick(READY - 6.0)
    third_hop(copies[0], waits[0])
    for dom in away[1:3]:
        for wait in waits:
            wait(dom)
        ready(dom)
    tick(READY - 4.0)
    third_hop(copies[1], waits[1])
    ready(diag)
    tick(READY - 2.0)
    for wait in waits:
        wait(away[3])
    ready(away[3])

    every = list(range(doms))
    held = [[0], [6, 7, 0, 1, 2]]
    busy = [[7, 0, 1], [5, 6, 7, 0, 1, 2, 3]]

    now = [READY]

    def spend(time):
        now[0] += time

    def advance(k):
        end = k == DEGREE
        source = held[k - 1] if k <= 2 else every
        active = busy[k - 1] if k <= 2 else every
        result = held[k] if k < 2 else every
        old = [] if k == 1 else held[k - 2] if k <= 3 else every
        store = odd if k % 2 else even
        for d in source:
            after, ahead = (d + 1) % doms, (d - 1) % doms
            for at, bases in ((0, (0, size)), (2 * size, (2 * size,))):
                g = mm(pick[d], pieces[d, at : at + owned]).astype(b16)
                for base in bases:
                    pieces[after, base + owned : base + owned + slots] = g[:slots]
                    pieces[ahead, base + owned + slots : base + size] = g[slots:]
        spend(0.05 * len(source))
        for d in active:
            after, ahead = (d + 1) % doms, (d - 1) % doms
            if k > 1:
                y = mm(matrix[d], pieces[d])
            elif d == 0:
                y = matrix[d, :, :owned].astype(jnp.float32) + matrix[d, :, size : size + owned].astype(jnp.float32)
            else:
                beyond = pieces[d, owned:size]
                y = mm(matrix[d, :, owned:size], beyond) + mm(matrix[d, :, size + owned : 2 * size], beyond)
            image[d] = y[:owned]
            high, low = high_low(y[owned:])
            ghosts[ahead, :slots] = high[:slots]
            ghosts[ahead, 2 * slots : 3 * slots] = low[:slots]
            ghosts[after, slots : 2 * slots] = high[slots:]
            ghosts[after, 3 * slots :] = low[slots:]
            spend(0.28 if k > 1 else 0.1)
            if d in (CLOSE if k >= DEGREE - 1 else STOPS):
                tick(now[0])
        for d in result:
            home = slice(d * owned, (d + 1) * owned)
            y = mm(spread[d], ghosts[d])
            if d in active:
                y = y + image[d]
            v = y if k == 1 else 2.0 * y
            if d in old:
                v = v - store[home]
            if end:
                for first, count in SPAN:
                    at = doms * first + d * count
                    odd[at : at + count] = v[first : first + count]
            else:
                store[home] = v
                high, low = high_low(v)
                pieces[d, :owned] = high
                pieces[d, size : size + owned] = high
                pieces[d, 2 * size : 2 * size + owned] = low
        spend(0.055 * len(result))

    for k in range(1, DEGREE + 1):
        advance(k)
    tick(1000.0)
    for d in range(doms):
        high, low = high_low(jnp.transpose(odd[d * owned : (d + 1) * owned]))
        p_high[:, d * owned : (d + 1) * owned] = high
        p_low[:, d * owned : (d + 1) * owned] = low

    def product(at):
        high, low = y_high[at], y_low[at]
        return mm(p_high[:, at], high) + (mm(p_high[:, at], low) + mm(p_low[:, at], high))

    bulk = doms * SPAN[-2][0]
    for _, act, details in late[:2]:
        act(*details)
    out[...] = product(slice(0, bulk))
    for _, act, details in late[2:]:
        act(*details)
    out[...] = out[...] + product(slice(bulk, doms * owned))

    for copy in unsent:
        copy.wait_send()
    for j in range(bands):
        for c in range(len(SPAN)):
            @pl.when(z < j)
            def _():
                to_right(j, c).wait_send()

            @pl.when(z > j)
            def _():
                to_left(j, c).wait_send()


def fused(waves, cell_matrix, connect, send_index, rotation):
    owned, width = waves.shape
    slots = send_index.shape[2]
    bands = lax.axis_size("band")
    size = owned + 2 * slots
    doms = 8
    vmem = pl.BlockSpec(memory_space=pltpu.VMEM)
    anywhere = pl.BlockSpec(memory_space=pl.ANY)
    cells = jnp.swapaxes(cell_matrix, 0, 1)
    f32, b16 = jnp.float32, jnp.bfloat16
    dma = pltpu.SemaphoreType.DMA
    return pl.pallas_call(
        functools.partial(fused_kernel, bands, owned, slots),
        out_shape=jax.ShapeDtypeStruct((owned, width), f32),
        in_specs=[anywhere, anywhere, vmem, vmem, anywhere],
        out_specs=vmem,
        scratch_shapes=[
            pltpu.VMEM((owned, width), f32),
            pltpu.VMEM(cells.shape, f32),
            pltpu.VMEM(rotation.shape, f32),
            dma((bands + 2,)),
            pltpu.VMEM((bands, owned, width), f32),
            pltpu.VMEM((bands, owned, width), f32),
            pltpu.VMEM((bands, owned, width), f32),
            pltpu.VMEM((doms, HALVES[1][0] + HALVES[1][1], size), f32),
            pltpu.VMEM((doms, size, 3 * size), b16),
            pltpu.VMEM((doms, 2 * slots, owned), b16),
            pltpu.VMEM((doms, owned, 4 * slots), b16),
            pltpu.VMEM((doms, 3 * size, owned), b16),
            pltpu.VMEM((doms, 4 * slots, owned), b16),
            pltpu.VMEM((doms, owned, owned), f32),
            pltpu.VMEM((doms * owned, owned), f32),
            pltpu.VMEM((doms * owned, owned), f32),
            pltpu.VMEM((doms, owned, width), f32),
            pltpu.VMEM((doms * owned, width), b16),
            pltpu.VMEM((doms * owned, width), b16),
            pltpu.VMEM((owned, doms * owned), b16),
            pltpu.VMEM((owned, doms * owned), b16),
            dma((bands, len(SPAN))), dma((bands, len(SPAN))), dma((bands, len(SPAN))),
            dma((2, 7)), dma((2, doms)),
            dma((len(SPAN), 7)), dma((len(SPAN), doms)),
        ],
        compiler_params=pltpu.CompilerParams(
            vmem_limit_bytes=60 * 2**20, collective_id=0, has_side_effects=True),
        cost_estimate=pl.CostEstimate(
            flops=DEGREE * doms * 6 * size * size * owned, bytes_accessed=2**24, transcendentals=0),
    )(waves, cells, connect, send_index, rotation)


def shards(waves, cell_matrix, connect, send_index, rotation):
    owned = waves.shape[0]
    width = waves.shape[1]
    slots = send_index.shape[2]
    doms = lax.axis_size("dom")
    if doms == 8 and width == doms * LANES // 2 and 2 * slots == LANES and owned == 2 * LANES and lax.axis_size("band") == 4:
        return fused(waves, cell_matrix, connect, send_index, rotation)
    size = owned + 2 * slots
    seat = jax.nn.one_hot(connect, size, dtype=jnp.float32)
    half_way = jnp.einsum("cij,cjn->cin", cell_matrix, seat, precision=lax.Precision.HIGH)
    local = jnp.einsum("cim,cin->mn", seat, half_way, precision=lax.Precision.HIGH)
    node = jnp.arange(size)
    shift = jnp.where((node[:, None] == node[None, :]) & (node[:, None] < owned), centre, 0.0)
    local = (local - shift) / half_width
    row = jnp.zeros((8, size), jnp.float32).at[0, : 2 * slots].set(
        send_index.reshape(-1).astype(jnp.float32)
    )
    everyone = lax.all_gather(jnp.concatenate([local, row], axis=0), "dom")
    high, low = split(everyone[:, :size])
    index = everyone[:, size, : 2 * slots].astype(jnp.int32)
    pick = jax.nn.one_hot(index, owned, dtype=jnp.bfloat16)
    spread = jnp.swapaxes(pick, 1, 2)

    partial = jnp.dot(waves, rotation, precision=lax.Precision.HIGH, preferred_element_type=jnp.float32)
    turned = lax.psum_scatter(partial, "band", scatter_dimension=1, tiled=True)
    share = width // doms
    columns = lax.all_to_all(turned, "dom", split_axis=1, concat_axis=0, tiled=True)
    columns = columns.reshape(doms, owned, share)
    half = LANES // 2
    columns = jnp.pad(columns, ((0, 0), (0, 0), (0, half - share)))
    columns = jnp.concatenate([columns, columns], axis=2)
    vmem = pl.BlockSpec(memory_space=pltpu.VMEM)
    done = pl.pallas_call(
        functools.partial(filter_kernel, doms, owned, slots, half),
        out_shape=jax.ShapeDtypeStruct((doms, owned, LANES), jnp.float32),
        in_specs=[vmem] * 5,
        out_specs=vmem,
        scratch_shapes=[
            pltpu.VMEM((doms, size, LANES), jnp.bfloat16),
            pltpu.VMEM((doms, 2 * slots, LANES), jnp.bfloat16),
            pltpu.VMEM((doms, owned, LANES), jnp.float32),
            pltpu.VMEM((doms, owned, LANES), jnp.float32),
        ],
        compiler_params=pltpu.CompilerParams(vmem_limit_bytes=56 * 2**20),
        cost_estimate=pl.CostEstimate(
            flops=DEGREE * doms * 4 * size * size * LANES, bytes_accessed=2**24, transcendentals=0
        ),
    )(high, low, pick, spread, columns)
    back = done[:, :, :share].reshape(doms * owned, share)
    return lax.all_to_all(back, "dom", split_axis=0, concat_axis=1, tiled=True)


def solution(mesh):
    in_specs = (
        P("dom", "band"),
        P("dom", None, None),
        P("dom", None),
        P("dom", None, None),
        P("band", None),
    )
    out_specs = P("dom", "band")
    return jax.shard_map(shards, mesh=mesh, in_specs=in_specs, out_specs=out_specs, check_vma=False)
```
